256 devices in a mesh: ctx: 64 (over x_lo, z, y), fsdp: 4 (over x_hi, core).
Axes of the slice: x: 4 (x_hi: 2, x_lo: 2; x = x_hi * 2 + x_lo), y: 4, z: 8, core: 2. Of those that a mesh axis runs over, the one named last changes fastest.
Arguments:
- q_raw: bfloat16 [8192, 2560], P('ctx', 'fsdp'), may hold values from -3000 to 3000
- k_raw: bfloat16 [8192, 2560], P('ctx', 'fsdp'), may hold values from -3000 to 3000
- values: bfloat16 [8192, 2560], P('ctx', 'fsdp'), may hold values from -6 to 6
- positions: int32 [8192, 3], P('ctx'), may hold values from 0 to 79, as said below
- cotangent: bfloat16 [8192, 5120], P('ctx'), may hold values from -6 to 6
- out_weight: bfloat16 [2560, 5120], P('fsdp'), may hold values from -0.078125 to 0.078125
- modulation: float32 [50, 5120], replicated, may hold values from -4 to 4
- step_index: int32 [1], replicated, may hold values from 0 to 49
Outputs:
- query_grad: bfloat16 [8192, 2560], P('ctx', 'fsdp')
- key_grad: bfloat16 [8192, 2560], P('ctx', 'fsdp')
- value_grad: bfloat16 [8192, 2560], P('ctx', 'fsdp')
The draws below stay inside these ranges and needn't reach their ends.
Inputs may be any that keep to these rules, and one draw needn't show every extreme that they name: `positions`: frame, row and column coordinates of each token in the latent grid.
All inputs are finite; a program needn't handle non-finite values.
Results may differ from the reference program's by a relative error of at most 0.034.
Values may be sent and summed in bfloat16 or wider, within the bound.
No kernel may reach another device: no remote copies, remote signals or barrier semaphores. Data moves between devices by JAX's collectives and lax.ppermute only.
A program may use at most 192 MiB of HBM per device.

```python
import math
import jax
import jax.numpy as jnp
import numpy as np
from jax import lax

D = 5120
HEAD_DIM = 128
TOK_DEV = 128
STEPS = 50
HEADS = 20
INNER = 2560
TOKENS = 8192


value_limit = 3000.0


overall = 0.05


def angle_table_drawn(head_size):
    side_dim = 2 * (head_size // 6)
    first_dim = head_size - 2 * side_dim
    freq_table = np.zeros((3, head_size // 2), np.float32)
    column = 0
    for axis_number, group_dim in enumerate([first_dim, side_dim, side_dim]):
        for pair_index in range(group_dim // 2):
            freq_table[axis_number, column] = 10000.0 ** (-2.0 * pair_index / group_dim)
            column += 1
    return freq_table


def grid_positions(key):
    base_key = jax.random.fold_in(key, 101)
    frame_key, height_key, width_key = jax.random.split(base_key, 3)
    frames = jax.random.randint(frame_key, (TOKENS,), 0, 21)
    heights = jax.random.randint(height_key, (TOKENS,), 0, 45)
    widths = jax.random.randint(width_key, (TOKENS,), 0, 80)
    widths = jnp.where(jnp.arange(TOKENS) == 0, 79, widths)
    return jnp.stack([frames, heights, widths], axis=1).astype(jnp.int32)


def block_shared(key):
    shared = jax.random.normal(jax.random.fold_in(key, 102), (TOKENS // TOK_DEV, INNER), jnp.float32)
    return jnp.repeat(shared, TOK_DEV, axis=0)


def feature_rows(own_key, shared_rows, rise_factor):
    normal_key = jax.random.fold_in(own_key, 0)
    column_key = jax.random.fold_in(own_key, 2)
    row_key = jax.random.fold_in(own_key, 3)
    gaussian = jax.random.normal(normal_key, (TOKENS, INNER), jnp.float32)
    mixture = gaussian
    ramp_values = jnp.arange(INNER, dtype=jnp.float32) / INNER
    columns = jnp.exp(ramp_values * math.log(rise_factor) + jax.random.uniform(column_key, (INNER,), jnp.float32) * math.log(10.0 / 3.0))
    row_scale = jnp.exp(jax.random.uniform(row_key, (TOKENS, 1), jnp.float32) * math.log(10.0))
    return overall * row_scale * columns[None, :] * (mixture + 0.6 * shared_rows)


def chosen_rows():
    amplitudes = [12.0, 25.0, 50.0, 120.0]
    count_rows = min(4, TOKENS // TOK_DEV)
    return [(index_value * TOK_DEV, (3 * index_value + 1) % HEADS, amplitudes[index_value]) for index_value in range(count_rows)]


def query_values(key, rise_factor):
    queries = feature_rows(jax.random.fold_in(key, 103), block_shared(key), rise_factor)
    return jnp.clip(queries, -value_limit, value_limit)


def draw_positions(key, part):
    return grid_positions(key)


def draw_q_raw(key, part):
    rise_factor = 3.0
    return query_values(key, rise_factor).astype(jnp.bfloat16)


def draw_k_raw(key, part):
    rise_factor, boost_weight = (3.0, 0.0)
    queries = query_values(key, rise_factor)
    positions = grid_positions(key)
    shared_rows = block_shared(key)
    key = jax.random.fold_in(key, 104)
    keys = jnp.clip(feature_rows(key, shared_rows, rise_factor), -value_limit, value_limit)
    angles = jnp.dot(positions.astype(jnp.float32), jnp.asarray(angle_table_drawn(HEAD_DIM)), precision=lax.Precision.HIGHEST)
    token_ids = jnp.arange(TOKENS)[:, None]
    head_ids = jnp.arange(INNER) // HEAD_DIM
    column_ids = jnp.arange(INNER)
    for row_index, head_index, amplitude in chosen_rows():
        row_query = queries[row_index]
        turned = jnp.repeat(angles[row_index] - angles[row_index + 1], 2)
        cosine = jnp.tile(jnp.cos(turned), HEADS)
        sine_signed = jnp.tile(jnp.sin(turned), HEADS) * jnp.where(column_ids % 2 == 0, -1.0, 1.0)
        partner = jnp.where(column_ids % 2 == 0, jnp.roll(row_query, -1), jnp.roll(row_query, 1))
        rotated = row_query * cosine + partner * sine_signed
        in_head = head_ids == head_index
        energy_head = jnp.sum(jnp.where(in_head, row_query * row_query, 0.0))
        energy_rest = jnp.sum(jnp.where(in_head, 0.0, row_query * row_query))
        score_one = energy_head / (energy_head + energy_rest) * INNER / math.sqrt(HEAD_DIM)
        ratio = score_one / jnp.maximum(score_one - 2.0, 0.5 * score_one)
        spread = jnp.sqrt(jnp.maximum((ratio * ratio * (energy_head + energy_rest) - energy_head) / energy_rest, 1.0))
        neighbour = jnp.where(in_head, rotated, spread * row_query)
        keys = jnp.where(token_ids == row_index, 1.0 * keys + boost_weight * row_query[None, :], keys)
        keys = jnp.where(token_ids == row_index + 1, 1.0 * keys + boost_weight * neighbour[None, :], keys)
    return jnp.clip(keys, -value_limit, value_limit).astype(jnp.bfloat16)


def levels(stream_key, shape, cuts, low, top_value):
    def one(position, parts):
        steps = jax.random.uniform(jax.random.fold_in(jax.random.fold_in(stream_key, 6), position), (parts,), jnp.float32, low / len(cuts), top_value / len(cuts))
        return jnp.repeat(jnp.exp(steps), shape[position] // parts).reshape((-1,) + (1,) * (len(shape) - position - 1))

    loudness = one(*cuts[0])
    for cut in cuts[1:]:
        loudness = loudness * one(*cut)
    return loudness


def noise(stream_key, extent, scale, reach, cuts=(), kind=jnp.bfloat16):
    loudness = levels(stream_key, extent, cuts, -0.22, 0.18) if cuts else 1.0
    values = jax.random.normal(stream_key, extent, jnp.float32) * scale * loudness
    return jnp.minimum(jnp.maximum(values, -reach), reach).astype(kind)


def setup_inputs(seed: int = 0) -> dict:
    splits = jax.random.split(jax.random.key(seed), 9)
    return {
        "q_raw": draw_q_raw(jax.random.fold_in(splits[8], 71), 0),
        "k_raw": draw_k_raw(jax.random.fold_in(splits[8], 71), 0),
        "values": noise(splits[2], (TOKENS, INNER), 1.0, 6.0, ((0, 64), (1, 4))),
        "positions": draw_positions(jax.random.fold_in(splits[8], 71), 0),
        "cotangent": noise(splits[4], (TOKENS, D), 1.0, 6.0, ((0, 64),)),
        "out_weight": noise(splits[5], (INNER, D), D ** -0.5, 0.078125, ((0, 4),)),
        "modulation": noise(splits[6], (STEPS, D), 1.0, 4.0, (), jnp.float32),
        "step_index": jax.random.randint(splits[7], (1,), 0, STEPS).astype(jnp.int32),
    }


EPSILON = 1e-06

def angle_table(head_size):
    side_dim = 2 * (head_size // 6)
    first_dim = head_size - 2 * side_dim
    freq_table = np.zeros((3, head_size // 2), np.float32)
    column = 0
    for axis_number, group_dim in enumerate([first_dim, side_dim, side_dim]):
        for pair_index in range(group_dim // 2):
            freq_table[axis_number, column] = 10000.0 ** (-2.0 * pair_index / group_dim)
            column += 1
    return freq_table

def rotation(positions, heads_count, head_size):
    angles = jnp.dot(positions.astype(jnp.float32), jnp.asarray(angle_table(head_size)), precision=lax.Precision.HIGHEST)
    doubled = jnp.repeat(angles, 2, axis=1)
    cosine = jnp.tile(jnp.cos(doubled), (1, heads_count))
    sine_full = jnp.tile(jnp.sin(doubled), (1, heads_count))
    parity = jnp.tile(jnp.array([-1.0, 1.0], jnp.float32), heads_count * head_size // 2)
    return (cosine, sine_full * parity[None, :])

def rotate(source, cosine, signed_sine, direction):
    column_ids = jnp.arange(source.shape[1])
    partner = jnp.where(column_ids % 2 == 0, jnp.roll(source, -1, axis=1), jnp.roll(source, 1, axis=1))
    return source * cosine + direction * partner * signed_sine

def reference(q_raw, k_raw, values, positions, cotangent, out_weight, modulation, step_index):
    heads_count = q_raw.shape[1] // HEAD_DIM
    scaling = 1.0 / math.sqrt(HEAD_DIM)
    gate_row = lax.dynamic_index_in_dim(modulation, step_index[0], 0, keepdims=False)
    gated_cot = (gate_row[None, :] * cotangent.astype(jnp.float32)).astype(jnp.bfloat16)
    attn_cot = jnp.dot(gated_cot, out_weight.T, preferred_element_type=jnp.float32).astype(jnp.bfloat16)
    cosine, signed_sine = rotation(positions, heads_count, HEAD_DIM)
    q_float = q_raw.astype(jnp.float32)
    k_float = k_raw.astype(jnp.float32)
    q_inverse = lax.rsqrt(lax.optimization_barrier(jnp.mean(q_float * q_float, axis=1)) + EPSILON)
    k_inverse = lax.rsqrt(lax.optimization_barrier(jnp.mean(k_float * k_float, axis=1)) + EPSILON)
    q_normed = q_float * q_inverse[:, None]
    k_normed = k_float * k_inverse[:, None]
    q_rot = rotate(q_normed, cosine, signed_sine, 1.0).astype(jnp.bfloat16)
    k_rot = rotate(k_normed, cosine, signed_sine, 1.0).astype(jnp.bfloat16)

    def split_heads(matrix):
        return jnp.transpose(matrix.reshape(matrix.shape[0], heads_count, HEAD_DIM), (1, 0, 2))

    def join_heads(tensor):
        return jnp.transpose(tensor, (1, 0, 2)).reshape(tensor.shape[1], tensor.shape[0] * tensor.shape[2])

    def one_head(operands):
        query_h, key_h, value_h, cot_h = operands
        scores = jnp.dot(query_h, key_h.T, preferred_element_type=jnp.float32) * scaling
        row_top = lax.optimization_barrier(jnp.max(scores, axis=1, keepdims=True))
        log_total = row_top + jnp.log(lax.optimization_barrier(jnp.sum(jnp.exp(scores - row_top), axis=1, keepdims=True)))
        probs_full = jnp.exp(scores - log_total)
        probs_low = probs_full.astype(jnp.bfloat16)
        grad_prob = jnp.dot(cot_h, value_h.T, preferred_element_type=jnp.float32)
        row_delta = lax.optimization_barrier(jnp.sum(probs_full * grad_prob, axis=1, keepdims=True))
        weighted = (probs_full * grad_prob).astype(jnp.bfloat16)
        first_term = jnp.dot(weighted, key_h, preferred_element_type=jnp.float32)
        second_term = jnp.dot(probs_low, key_h, preferred_element_type=jnp.float32)
        dq_rot = (first_term - row_delta * second_term) * scaling
        dscore = (probs_full * (grad_prob - row_delta)).astype(jnp.bfloat16)
        dk_rot = jnp.dot(dscore.T, query_h, preferred_element_type=jnp.float32) * scaling
        value_grad = jnp.dot(probs_low.T, cot_h, preferred_element_type=jnp.float32).astype(jnp.bfloat16)
        return (dq_rot, dk_rot, value_grad)
    dq_heads, dk_heads, dv_heads = lax.map(one_head, (split_heads(q_rot), split_heads(k_rot), split_heads(values), split_heads(attn_cot)))
    dq_normed = rotate(join_heads(dq_heads), cosine, signed_sine, -1.0)
    dk_normed = rotate(join_heads(dk_heads), cosine, signed_sine, -1.0)
    q_slope = lax.optimization_barrier(jnp.mean(dq_normed * q_normed, axis=1, keepdims=True))
    k_slope = lax.optimization_barrier(jnp.mean(dk_normed * k_normed, axis=1, keepdims=True))
    query_grad = (q_inverse[:, None] * (dq_normed - q_normed * q_slope)).astype(jnp.bfloat16)
    key_grad = (k_inverse[:, None] * (dk_normed - k_normed * k_slope)).astype(jnp.bfloat16)
    return (query_grad, key_grad, join_heads(dv_heads))
```

```python
import math

import jax
import jax.numpy as jnp
import numpy as np
from jax import lax
from jax.experimental import pallas as pl
from jax.experimental.pallas import tpu as pltpu
from jax.sharding import Mesh
from jax.sharding import PartitionSpec as P

HEAD_DIM = 128
EPSILON = 1e-06
LOG2E = math.log2(math.e)
SCALING = 1.0 / math.sqrt(HEAD_DIM)
TOKENS_AXES = ("xl", "z", "y")
HEADS_AXES = ("xh", "c")
VMEM_LIMIT = 48 * 1024 * 1024
NT = (((1,), (1,)), ((), ()))
TN = (((0,), (0,)), ((), ()))


def angle_table(head_size):
    side_dim = 2 * (head_size // 6)
    first_dim = head_size - 2 * side_dim
    freq_table = np.zeros((3, head_size // 2), np.float32)
    column = 0
    for axis_number, group_dim in enumerate([first_dim, side_dim, side_dim]):
        for pair_index in range(group_dim // 2):
            freq_table[axis_number, column] = 10000.0 ** (-2.0 * pair_index / group_dim)
            column += 1
    return freq_table


def rotation(positions, heads_count):
    angles = jnp.dot(
        positions.astype(jnp.float32),
        jnp.asarray(np.repeat(angle_table(HEAD_DIM), 2, axis=1)),
        precision=lax.Precision.HIGHEST,
    )
    parity = jnp.tile(jnp.array([-1.0, 1.0], jnp.float32), HEAD_DIM // 2)
    cosine = jnp.cos(angles)
    signed_sine = jnp.sin(angles) * parity[None, :]
    return jnp.tile(cosine, (1, heads_count)), jnp.tile(signed_sine, (1, heads_count))


def rotate(source, cosine, signed_sine, direction):
    column_ids = jnp.arange(source.shape[1])
    partner = jnp.where(
        column_ids % 2 == 0, jnp.roll(source, -1, axis=1), jnp.roll(source, 1, axis=1)
    )
    return source * cosine + direction * partner * signed_sine


def shift(x, axis, distance):
    size = lax.axis_size(axis)
    return lax.ppermute(x, axis, [(i, (i + distance) % size) for i in range(size)])


def swap_core(x):
    return lax.ppermute(x, ("xl", "c"), [(0, 0), (1, 2), (2, 1), (3, 3)])


def blocks_of(refs, column):
    return jnp.concatenate([ref[:, pl.ds(column, HEAD_DIM)] for ref in refs], axis=0)


def stats_kernel(nq, nk, heads, *refs):
    query_refs, key_refs = refs[:nq], refs[nq : nq + nk]
    stats_ref, k_ref, v_ref = refs[nq + nk :]
    width = heads * HEAD_DIM
    stats_ref[...] = jnp.zeros_like(stats_ref)

    @pl.loop(0, heads)
    def _(h):
        col = pl.multiple_of(h * HEAD_DIM, HEAD_DIM)
        cot_col = pl.multiple_of(width + h * HEAD_DIM, HEAD_DIM)
        k_ref[...] = blocks_of(key_refs, col)
        v_ref[...] = blocks_of(key_refs, cot_col)
        for t in range(nq // 2):
            pair = query_refs[2 * t : 2 * t + 2]
            q = blocks_of(pair, col)
            cot = blocks_of(pair, cot_col)
            s = lax.dot_general(k_ref[...], q, NT, preferred_element_type=jnp.float32)
            g = lax.dot_general(v_ref[...], cot, NT, preferred_element_type=jnp.float32)
            s = s * (SCALING * LOG2E)
            top = jnp.max(s, axis=0, keepdims=True)
            e = jnp.exp2(s - top)
            cols = slice(t * 256, t * 256 + 256)
            stats_ref[pl.ds(h, 1), cols] = top
            stats_ref[pl.ds(8 + h, 1), cols] = jnp.sum(e, axis=0, keepdims=True)
            stats_ref[pl.ds(16 + h, 1), cols] = jnp.sum(e * g, axis=0, keepdims=True)


def grads_kernel(nq, nk, heads, *refs):
    query_refs, key_refs = refs[:nq], refs[nq : nq + nk]
    totals_ref = refs[nq + nk]
    outs = refs[nq + nk + 1 :]
    dq_refs, mine_ref, other_ref = outs[:nq], outs[nq], outs[nq + 1]
    k_ref, v_ref, dk_ref, dv_ref = outs[nq + 2 :]
    width = heads * HEAD_DIM
    half = nk // 2 * 128

    @pl.loop(0, heads)
    def _(h):
        col = pl.multiple_of(h * HEAD_DIM, HEAD_DIM)
        cot_col = pl.multiple_of(width + h * HEAD_DIM, HEAD_DIM)
        k_ref[...] = blocks_of(key_refs, col)
        v_ref[...] = blocks_of(key_refs, cot_col)
        for t in range(nq // 2):
            pair = query_refs[2 * t : 2 * t + 2]
            q = blocks_of(pair, col)
            cot = blocks_of(pair, cot_col)
            cols = slice(t * 256, t * 256 + 256)
            log_total = totals_ref[pl.ds(h, 1), cols]
            delta = totals_ref[pl.ds(8 + h, 1), cols]
            s = lax.dot_general(k_ref[...], q, NT, preferred_element_type=jnp.float32)
            g = lax.dot_general(v_ref[...], cot, NT, preferred_element_type=jnp.float32)
            p = jnp.exp2(s * (SCALING * LOG2E) - log_total)
            ds = (p * (g - delta)).astype(jnp.bfloat16)
            dv = jnp.dot(p.astype(jnp.bfloat16), cot, preferred_element_type=jnp.float32)
            dk = jnp.dot(ds, q, preferred_element_type=jnp.float32)
            if t == 0:
                dv_ref[...] = dv
                dk_ref[...] = dk
            else:
                dv_ref[...] += dv
                dk_ref[...] += dk
            dq = lax.dot_general(ds, k_ref[...], TN, preferred_element_type=jnp.float32)
            dq = (dq * SCALING).astype(jnp.bfloat16)
            dq_refs[2 * t][:, pl.ds(col, HEAD_DIM)] = dq[:128]
            dq_refs[2 * t + 1][:, pl.ds(col, HEAD_DIM)] = dq[128:]
        dk = (dk_ref[...] * SCALING).astype(jnp.bfloat16)
        dv = dv_ref[...].astype(jnp.bfloat16)
        mine_ref[:, pl.ds(col, HEAD_DIM)] = dk[:half]
        other_ref[:, pl.ds(col, HEAD_DIM)] = dk[half:]
        mine_ref[:, pl.ds(cot_col, HEAD_DIM)] = dv[:half]
        other_ref[:, pl.ds(cot_col, HEAD_DIM)] = dv[half:]


def block_stats(queries, keys, heads):
    nq, nk = len(queries), len(keys)
    vmem = pl.BlockSpec(memory_space=pltpu.VMEM)
    return pl.pallas_call(
        lambda *refs: stats_kernel(nq, nk, heads, *refs),
        out_shape=jax.ShapeDtypeStruct((24, nq * 128), jnp.float32),
        in_specs=[vmem] * (nq + nk),
        out_specs=vmem,
        scratch_shapes=[
            pltpu.VMEM((nk * 128, HEAD_DIM), jnp.bfloat16),
            pltpu.VMEM((nk * 128, HEAD_DIM), jnp.bfloat16),
        ],
        compiler_params=pltpu.CompilerParams(vmem_limit_bytes=VMEM_LIMIT),
        cost_estimate=pl.CostEstimate(
            flops=heads * nq * nk * 128 * 128 * 128 * 4,
            bytes_accessed=(nq + nk) * 128 * heads * 512,
            transcendentals=heads * nq * nk * 128 * 128,
        ),
        name="block_stats",
    )(*queries, *keys)


def block_grads(queries, keys, totals, heads):
    nq, nk = len(queries), len(keys)
    width = heads * HEAD_DIM
    vmem = pl.BlockSpec(memory_space=pltpu.VMEM)
    outs = pl.pallas_call(
        lambda *refs: grads_kernel(nq, nk, heads, *refs),
        out_shape=[jax.ShapeDtypeStruct((128, width), jnp.bfloat16)] * nq
        + [jax.ShapeDtypeStruct((nk // 2 * 128, 2 * width), jnp.bfloat16)] * 2,
        in_specs=[vmem] * (nq + nk + 1),
        out_specs=[vmem] * (nq + 2),
        scratch_shapes=[
            pltpu.VMEM((nk * 128, HEAD_DIM), jnp.bfloat16),
            pltpu.VMEM((nk * 128, HEAD_DIM), jnp.bfloat16),
            pltpu.VMEM((nk * 128, HEAD_DIM), jnp.float32),
            pltpu.VMEM((nk * 128, HEAD_DIM), jnp.float32),
        ],
        compiler_params=pltpu.CompilerParams(vmem_limit_bytes=VMEM_LIMIT),
        cost_estimate=pl.CostEstimate(
            flops=heads * nq * nk * 128 * 128 * 128 * 10,
            bytes_accessed=(nq + nk) * 128 * heads * 1024,
            transcendentals=heads * nq * nk * 128 * 128,
        ),
        name="block_grads",
    )(*queries, *keys, totals)
    return outs[:nq], outs[nq], outs[nq + 1]


def shift_stats(stats, distance):
    moved = shift(stats, "z", distance)
    return jnp.roll(moved, distance * 128, axis=1)


def merge(parts):
    top = parts[0][:8]
    for part in parts[1:]:
        top = jnp.maximum(top, part[:8])
    total = weight = 0.0
    for part in parts:
        factor = jnp.exp2(part[:8] - top)
        total = total + part[8:16] * factor
        weight = weight + part[16:] * factor
    return top, total, weight


def shards(q_raw, k_raw, values, positions, cotangent, out_weight, modulation, step_index):
    width = q_raw.shape[1]
    heads = width // HEAD_DIM
    inner_width = width * 4
    q_float = q_raw.astype(jnp.float32)
    k_float = k_raw.astype(jnp.float32)
    squares = jnp.stack(
        [jnp.sum(q_float * q_float, axis=1), jnp.sum(k_float * k_float, axis=1)]
    )
    squares = squares + shift(squares, "c", 1)
    squares = squares + shift(squares, "xh", 1)
    inverse = lax.rsqrt(squares / inner_width + EPSILON)
    gate_row = lax.dynamic_slice_in_dim(modulation, step_index[0], 1, 0)
    gated_cot = (gate_row * cotangent.astype(jnp.float32)).astype(jnp.bfloat16)
    attn_cot = lax.dot_general(
        gated_cot, out_weight, NT, preferred_element_type=jnp.float32
    ).astype(jnp.bfloat16)
    cosine, signed_sine = rotation(positions, heads)
    q_normed = q_float * inverse[0][:, None]
    k_normed = k_float * inverse[1][:, None]
    q_rot = rotate(q_normed, cosine, signed_sine, 1.0).astype(jnp.bfloat16)
    k_rot = rotate(k_normed, cosine, signed_sine, 1.0).astype(jnp.bfloat16)

    query_own = swap_core(jnp.concatenate([q_rot, attn_cot], axis=1))
    key_own = swap_core(jnp.concatenate([k_rot, values], axis=1))

    left, right = query_own, query_own
    from_left, from_right = [], []
    for _ in range(3):
        left, right = shift(left, "z", 1), shift(right, "z", -1)
        from_left.append(left)
        from_right.append(right)
    far = jnp.concatenate([shift(left[:64], "z", 1), shift(right[64:], "z", -1)], axis=0)
    queries = [query_own, *from_left, far, *from_right[::-1]]

    keys = [key_own] + [shift(key_own, "y", d) for d in (1, 2, 3)]
    keys = keys + [shift(block, "c", 1) for block in keys]

    stats = block_stats(queries, keys, heads)
    stats = jnp.concatenate(merge([stats, shift_stats(stats, 1)]), axis=0)
    top, total, weight = merge([stats] + [shift_stats(stats, d) for d in (2, -2, 4)])
    valid = jnp.arange(8)[:, None] < heads
    total = jnp.where(valid, total, 1.0)
    totals = jnp.concatenate([top + jnp.log2(total), weight / total], axis=0)

    dq, mine, other = block_grads(queries, keys, totals, heads)

    left, right = shift(dq[4][:64], "z", -1), shift(dq[4][64:], "z", 1)
    left = dq[3] + jnp.concatenate([left, jnp.zeros_like(left)], axis=0)
    right = dq[5] + jnp.concatenate([jnp.zeros_like(right), right], axis=0)
    left = dq[2] + shift(left, "z", -1)
    right = dq[6] + shift(right, "z", 1)
    left = dq[1] + shift(left, "z", -1)
    right = dq[7] + shift(right, "z", 1)
    f32 = jnp.float32
    dq_sum = dq[0].astype(f32) + shift(left, "z", -1).astype(f32) + shift(right, "z", 1).astype(f32)

    chip_sum = (mine.astype(f32) + shift(other, "c", 1).astype(f32)).astype(jnp.bfloat16)
    dkv_sum = chip_sum[:128].astype(f32)
    for d in (1, 2, 3):
        dkv_sum = dkv_sum + shift(chip_sum[128 * d : 128 * d + 128], "y", -d).astype(f32)

    slopes = jnp.stack(
        [
            jnp.sum(dq_sum * query_own[:, :width].astype(f32), axis=1),
            jnp.sum(dkv_sum[:, :width] * key_own[:, :width].astype(f32), axis=1),
        ]
    )
    slope_sum = 0.0
    for a in (0, 1):
        for b in (0, 1):
            perm = [
                (xl * 4 + xh * 2 + c, c * 4 + (xh ^ b) * 2 + (xl ^ a))
                for xl in (0, 1)
                for xh in (0, 1)
                for c in (0, 1)
            ]
            slope_sum = slope_sum + lax.ppermute(slopes, ("xl", "xh", "c"), perm)
    slope = slope_sum / inner_width

    packed = jnp.concatenate([dq_sum, dkv_sum], axis=1).astype(jnp.bfloat16)
    packed = swap_core(packed)
    dq_normed = rotate(packed[:, :width].astype(f32), cosine, signed_sine, -1.0)
    dk_normed = rotate(packed[:, width : 2 * width].astype(f32), cosine, signed_sine, -1.0)
    query_grad = inverse[0][:, None] * (dq_normed - q_normed * slope[0][:, None])
    key_grad = inverse[1][:, None] * (dk_normed - k_normed * slope[1][:, None])
    return (
        query_grad.astype(jnp.bfloat16),
        key_grad.astype(jnp.bfloat16),
        packed[:, 2 * width :],
    )


def solution(mesh):
    axes = ("xl", "z", "y", "xh", "c")
    fine = Mesh(np.asarray(mesh.devices).reshape(2, 8, 4, 2, 2), axes)
    split = P(TOKENS_AXES, HEADS_AXES)
    rows = P(TOKENS_AXES, None)
    return jax.shard_map(
        shards,
        mesh=fine,
        in_specs=(split, split, split, rows, rows, P(HEADS_AXES, None), P(), P()),
        out_specs=(split, split, split),
        check_vma=False,
    )
```

```python
import math

import jax
import jax.numpy as jnp
import numpy as np
from jax import lax
from jax.experimental import pallas as pl
from jax.experimental.pallas import tpu as pltpu
from jax.sharding import Mesh
from jax.sharding import PartitionSpec as P

HEAD_DIM = 128
EPSILON = 1e-06
LOG2E = math.log2(math.e)
SCALING = 1.0 / math.sqrt(HEAD_DIM)
TOKENS_AXES = ("xl", "z", "y")
HEADS_AXES = ("xh", "c")
VMEM_LIMIT = 48 * 1024 * 1024
NT = (((1,), (1,)), ((), ()))
TN = (((0,), (0,)), ((), ()))


def angle_table(head_size):
    side_dim = 2 * (head_size // 6)
    first_dim = head_size - 2 * side_dim
    freq_table = np.zeros((3, head_size // 2), np.float32)
    column = 0
    for axis_number, group_dim in enumerate([first_dim, side_dim, side_dim]):
        for pair_index in range(group_dim // 2):
            freq_table[axis_number, column] = 10000.0 ** (-2.0 * pair_index / group_dim)
            column += 1
    return freq_table


def rotation(positions, heads_count):
    angles = jnp.dot(
        positions.astype(jnp.float32),
        jnp.asarray(np.repeat(angle_table(HEAD_DIM), 2, axis=1)),
        precision=lax.Precision.HIGHEST,
    )
    parity = jnp.tile(jnp.array([-1.0, 1.0], jnp.float32), HEAD_DIM // 2)
    cosine = jnp.cos(angles)
    signed_sine = jnp.sin(angles) * parity[None, :]
    return jnp.tile(cosine, (1, heads_count)), jnp.tile(signed_sine, (1, heads_count))


def rotate(source, cosine, signed_sine, direction):
    column_ids = jnp.arange(source.shape[1])
    partner = jnp.where(
        column_ids % 2 == 0, jnp.roll(source, -1, axis=1), jnp.roll(source, 1, axis=1)
    )
    return source * cosine + direction * partner * signed_sine


def shift(x, axis, distance):
    size = lax.axis_size(axis)
    return lax.ppermute(x, axis, [(i, (i + distance) % size) for i in range(size)])


def flip(x, axis):
    return lax.ppermute(x, axis, [(0, 1), (1, 0)])


def sum_heads_axes(x):
    total = x
    for mask in (1, 2, 3):
        total = total + lax.ppermute(x, HEADS_AXES, [(i, i ^ mask) for i in range(4)])
    return total


def ring_gather(x):
    half = x.shape[0] // 2
    left, right = x, x
    from_left, from_right = [], []
    for _ in range(3):
        left, right = shift(left, "z", 1), shift(right, "z", -1)
        from_left.append(left)
        from_right.append(right)
    far = [shift(left[:half], "z", 1), shift(right[half:], "z", -1)]
    return [x, *from_left, *far, *from_right[::-1]]


def ring_reduce(blocks):
    half = blocks[4].shape[0] // 2
    low, high = shift(blocks[4][:half], "z", -1), shift(blocks[4][half:], "z", 1)
    left = blocks[3] + jnp.concatenate([low, jnp.zeros_like(low)], axis=0)
    right = blocks[5] + jnp.concatenate([jnp.zeros_like(high), high], axis=0)
    for near in (2, 1):
        left = blocks[near] + shift(left, "z", -1)
        right = blocks[8 - near] + shift(right, "z", 1)
    f32 = jnp.float32
    return (
        blocks[0].astype(f32)
        + shift(left, "z", -1).astype(f32)
        + shift(right, "z", 1).astype(f32)
    )


def fill(target, pieces, column):
    row = 0
    for first, count, ref in pieces:
        target[row : row + count, :] = ref[first : first + count, pl.ds(column, HEAD_DIM)]
        row += count


class Layout:
    def __init__(self, *sides):
        self.operands = []
        self.plans = []
        for side in sides:
            plan = []
            for piece in side:
                array, first, count = piece if isinstance(piece, tuple) else (piece, 0, piece.shape[0])
                for number, known in enumerate(self.operands):
                    if known is array:
                        break
                else:
                    number = len(self.operands)
                    self.operands.append(array)
                plan.append((first, count, number))
            self.plans.append(plan)

    def pieces(self, refs):
        return [[(first, count, refs[number]) for first, count, number in plan] for plan in self.plans]


def stats_kernel(layout, heads, *refs):
    count = len(layout.operands)
    sides = layout.pieces(refs[:count])
    stats_ref, *scratch = refs[count:]
    q_ref, c_ref, k_ref, v_ref = scratch
    stats_ref[...] = jnp.zeros_like(stats_ref)

    @pl.loop(0, heads)
    def _(h):
        col = pl.multiple_of(h * HEAD_DIM, HEAD_DIM)
        for target, pieces in zip(scratch, sides):
            fill(target, pieces, col)
        for t in range(4):
            cols = slice(t * 256, t * 256 + 256)
            s = lax.dot_general(k_ref[...], q_ref[cols, :], NT, preferred_element_type=jnp.float32)
            g = lax.dot_general(v_ref[...], c_ref[cols, :], NT, preferred_element_type=jnp.float32)
            s = s * (SCALING * LOG2E)
            top = jnp.max(s, axis=0, keepdims=True)
            e = jnp.exp2(s - top)
            stats_ref[pl.ds(h, 1), cols] = top
            stats_ref[pl.ds(8 + h, 1), cols] = jnp.sum(e, axis=0, keepdims=True)
            stats_ref[pl.ds(16 + h, 1), cols] = jnp.sum(e * g, axis=0, keepdims=True)


def grads_kernel(layout, heads, *refs):
    count = len(layout.operands)
    sides = layout.pieces(refs[:count])
    totals_ref = refs[count]
    outs = refs[count + 1 :]
    dq_refs, dk_refs, dv_refs = outs[:4], outs[4:12], outs[12:20]
    scratch = outs[20:24]
    q_ref, c_ref, k_ref, v_ref = scratch
    dk_ref, dv_ref = outs[24:]

    @pl.loop(0, heads)
    def _(h):
        col = pl.multiple_of(h * HEAD_DIM, HEAD_DIM)
        for target, pieces in zip(scratch, sides):
            fill(target, pieces, col)
        for t in range(4):
            cols = slice(t * 256, t * 256 + 256)
            log_total = totals_ref[pl.ds(h, 1), cols]
            delta = totals_ref[pl.ds(8 + h, 1), cols]
            s = lax.dot_general(k_ref[...], q_ref[cols, :], NT, preferred_element_type=jnp.float32)
            g = lax.dot_general(v_ref[...], c_ref[cols, :], NT, preferred_element_type=jnp.float32)
            p = jnp.exp2(s * (SCALING * LOG2E) - log_total)
            ds = (p * (g - delta)).astype(jnp.bfloat16)
            dv = jnp.dot(p.astype(jnp.bfloat16), c_ref[cols, :], preferred_element_type=jnp.float32)
            dk = jnp.dot(ds, q_ref[cols, :], preferred_element_type=jnp.float32)
            if t == 0:
                dv_ref[...] = dv
                dk_ref[...] = dk
            else:
                dv_ref[...] += dv
                dk_ref[...] += dk
            dq = lax.dot_general(ds, k_ref[...], TN, preferred_element_type=jnp.float32)
            dq_refs[t][:, pl.ds(col, HEAD_DIM)] = (dq * SCALING).astype(jnp.bfloat16)
        for b in range(8):
            rows = slice(b * 128, b * 128 + 128)
            dk_refs[b][:, pl.ds(col, HEAD_DIM)] = (dk_ref[rows, :] * SCALING).astype(jnp.bfloat16)
            dv_refs[b][:, pl.ds(col, HEAD_DIM)] = dv_ref[rows, :].astype(jnp.bfloat16)


def head_scratch():
    return [pltpu.VMEM((1024, HEAD_DIM), jnp.bfloat16)] * 4


def block_stats(layout, heads):
    vmem = pl.BlockSpec(memory_space=pltpu.VMEM)
    return pl.pallas_call(
        lambda *refs: stats_kernel(layout, heads, *refs),
        out_shape=jax.ShapeDtypeStruct((24, 1024), jnp.float32),
        in_specs=[vmem] * len(layout.operands),
        out_specs=vmem,
        scratch_shapes=head_scratch(),
        compiler_params=pltpu.CompilerParams(vmem_limit_bytes=VMEM_LIMIT),
        cost_estimate=pl.CostEstimate(
            flops=heads * 2**27 * 4, bytes_accessed=2**23, transcendentals=heads * 2**20
        ),
        name="block_stats",
    )(*layout.operands)


def block_grads(layout, totals, heads):
    width = heads * HEAD_DIM
    vmem = pl.BlockSpec(memory_space=pltpu.VMEM)
    outs = pl.pallas_call(
        lambda *refs: grads_kernel(layout, heads, *refs),
        out_shape=[jax.ShapeDtypeStruct((256, width), jnp.bfloat16)] * 4
        + [jax.ShapeDtypeStruct((128, width), jnp.bfloat16)] * 16,
        in_specs=[vmem] * (len(layout.operands) + 1),
        out_specs=[vmem] * 20,
        scratch_shapes=head_scratch() + [pltpu.VMEM((1024, HEAD_DIM), jnp.float32)] * 2,
        compiler_params=pltpu.CompilerParams(vmem_limit_bytes=VMEM_LIMIT),
        cost_estimate=pl.CostEstimate(
            flops=heads * 2**27 * 10, bytes_accessed=2**24, transcendentals=heads * 2**20
        ),
        name="block_grads",
    )(*layout.operands, totals)
    return outs[:4], outs[4:12], outs[12:20]


def merge(parts):
    top = parts[0][:8]
    for part in parts[1:]:
        top = jnp.maximum(top, part[:8])
    total = weight = 0.0
    for part in parts:
        factor = jnp.exp2(part[:8] - top)
        total = total + part[8:16] * factor
        weight = weight + part[16:] * factor
    return top, total, weight


def shards(q_raw, k_raw, values, positions, cotangent, out_weight, modulation, step_index):
    width = q_raw.shape[1]
    heads = width // HEAD_DIM
    inner_width = width * 4
    f32 = jnp.float32
    value_blocks = ring_gather(values)
    q_float = q_raw.astype(f32)
    k_float = k_raw.astype(f32)
    squares = jnp.stack(
        [jnp.sum(q_float * q_float, axis=1), jnp.sum(k_float * k_float, axis=1)]
    )
    inverse = lax.rsqrt(sum_heads_axes(squares) / inner_width + EPSILON)
    cosine, signed_sine = rotation(positions, heads)
    q_normed = q_float * inverse[0][:, None]
    k_normed = k_float * inverse[1][:, None]
    q_rot = rotate(q_normed, cosine, signed_sine, 1.0).astype(jnp.bfloat16)
    k_rot = rotate(k_normed, cosine, signed_sine, 1.0).astype(jnp.bfloat16)
    gate_row = lax.dynamic_slice_in_dim(modulation, step_index[0], 1, 0)
    gated_cot = (gate_row * cotangent.astype(f32)).astype(jnp.bfloat16)
    attn_cot = lax.dot_general(
        gated_cot, out_weight, NT, preferred_element_type=f32
    ).astype(jnp.bfloat16)

    key_blocks = ring_gather(k_rot)

    q_flipped = flip(q_rot, "xl")
    q_pair = jnp.concatenate([q_rot, q_flipped], axis=0)
    q_left, q_right = shift(q_pair, "y", 1), shift(q_pair, "y", -1)
    q_far = [shift(q_left[:128], "y", 1), shift(q_right[128:], "y", -1)]
    queries = [q_pair, q_left, *q_far, q_right]
    cot_left, cot_right = shift(attn_cot, "y", 1), shift(attn_cot, "y", -1)
    near = jnp.concatenate([attn_cot, cot_left, cot_right], axis=0)
    near_flipped = flip(near, "xl")
    far = jnp.concatenate(
        [shift(cot_left[:64], "y", 1), shift(cot_right[64:], "y", -1)], axis=0
    )
    far_flipped = flip(far, "xl")
    cots = [
        (near, 0, 128),
        (near_flipped, 0, 128),
        (near, 128, 128),
        (near_flipped, 128, 128),
        far,
        far_flipped,
        (near, 256, 128),
        (near_flipped, 256, 128),
    ]
    layout = Layout(queries, cots, key_blocks, value_blocks)

    stats = block_stats(layout, heads)
    flipped = flip(stats, "xl").reshape(24, 4, 2, 128)[:, :, ::-1].reshape(24, 1024)
    stats = jnp.concatenate(merge([stats, flipped]), axis=0)
    parts = [jnp.roll(shift(stats, "y", d), 256 * d, axis=1) for d in (1, 2, 3)]
    top, total, weight = merge([stats] + parts)
    valid = jnp.arange(8)[:, None] < heads
    total = jnp.where(valid, total, 1.0)
    totals = jnp.concatenate([top + jnp.log2(total), weight / total], axis=0)

    dq, dk, dv = block_grads(layout, totals, heads)

    low, high = shift(dq[2][:128], "y", -1), shift(dq[2][128:], "y", 1)
    left = dq[1] + jnp.concatenate([low, jnp.zeros_like(low)], axis=0)
    right = dq[3] + jnp.concatenate([jnp.zeros_like(high), high], axis=0)
    dq_pair = (
        dq[0].astype(f32) + shift(left, "y", -1).astype(f32) + shift(right, "y", 1).astype(f32)
    )
    dq_sum = dq_pair[:128] + flip(dq_pair[128:].astype(jnp.bfloat16), "xl").astype(f32)
    dq_normed = rotate(dq_sum, cosine, signed_sine, -1.0)
    q_slope = sum_heads_axes(jnp.sum(dq_normed * q_normed, axis=1)) / inner_width
    query_grad = inverse[0][:, None] * (dq_normed - q_normed * q_slope[:, None])

    dk_sum = ring_reduce(dk)
    dk_normed = rotate(dk_sum, cosine, signed_sine, -1.0)
    k_slope = sum_heads_axes(jnp.sum(dk_normed * k_normed, axis=1)) / inner_width
    key_grad = inverse[1][:, None] * (dk_normed - k_normed * k_slope[:, None])
    dv_sum = ring_reduce(dv)
    return (
        query_grad.astype(jnp.bfloat16),
        key_grad.astype(jnp.bfloat16),
        dv_sum.astype(jnp.bfloat16),
    )


def solution(mesh):
    axes = ("xl", "z", "y", "xh", "c")
    fine = Mesh(np.asarray(mesh.devices).reshape(2, 8, 4, 2, 2), axes)
    split = P(TOKENS_AXES, HEADS_AXES)
    rows = P(TOKENS_AXES, None)
    return jax.shard_map(
        shards,
        mesh=fine,
        in_specs=(split, split, split, rows, rows, P(HEADS_AXES, None), P(), P()),
        out_specs=(split, split, split),
        check_vma=False,
    )
```

```python
import functools
import math

import jax
import jax.numpy as jnp
import numpy as np
from jax import lax
from jax.experimental import pallas as pl
from jax.experimental.pallas import tpu as pltpu
from jax.sharding import Mesh
from jax.sharding import PartitionSpec as P

HEAD_DIM = 128
EPSILON = 1e-06
LOG2E = math.log2(math.e)
SCALING = 1.0 / math.sqrt(HEAD_DIM)
TOKENS_AXES = ("xl", "z", "y")
HEADS_AXES = ("xh", "c")
VMEM_LIMIT = 58 * 1024 * 1024
NT = (((1,), (1,)), ((), ()))
TN = (((0,), (0,)), ((), ()))


def angle_table(head_size):
    side_dim = 2 * (head_size // 6)
    first_dim = head_size - 2 * side_dim
    freq_table = np.zeros((3, head_size // 2), np.float32)
    column = 0
    for axis_number, group_dim in enumerate([first_dim, side_dim, side_dim]):
        for pair_index in range(group_dim // 2):
            freq_table[axis_number, column] = 10000.0 ** (-2.0 * pair_index / group_dim)
            column += 1
    return freq_table


def rotation(positions, heads_count):
    angles = jnp.dot(
        positions.astype(jnp.float32),
        jnp.asarray(np.repeat(angle_table(HEAD_DIM), 2, axis=1)),
        precision=lax.Precision.HIGHEST,
    )
    parity = jnp.tile(jnp.array([-1.0, 1.0], jnp.float32), HEAD_DIM // 2)
    cosine = jnp.cos(angles)
    signed_sine = jnp.sin(angles) * parity[None, :]
    return jnp.tile(cosine, (1, heads_count)), jnp.tile(signed_sine, (1, heads_count))


def rotate(source, cosine, signed_sine, direction):
    column_ids = jnp.arange(source.shape[1])
    partner = jnp.where(
        column_ids % 2 == 0, jnp.roll(source, -1, axis=1), jnp.roll(source, 1, axis=1)
    )
    return source * cosine + direction * partner * signed_sine


def shift(x, axis, distance):
    size = lax.axis_size(axis)
    return lax.ppermute(x, axis, [(i, (i + distance) % size) for i in range(size)])


def flip(x, axis):
    return lax.ppermute(x, axis, [(0, 1), (1, 0)])


def sum_heads_axes(x):
    total = x
    for mask in (1, 2, 3):
        total = total + lax.ppermute(x, HEADS_AXES, [(i, i ^ mask) for i in range(4)])
    return total


def ring_gather(x):
    half = x.shape[0] // 2
    left, right = x, x
    from_left, from_right = [], []
    for _ in range(3):
        left, right = shift(left, "z", 1), shift(right, "z", -1)
        from_left.append(left)
        from_right.append(right)
    far = [shift(left[:half], "z", 1), shift(right[half:], "z", -1)]
    return [[x], *[[b] for b in from_left], far, *[[b] for b in from_right[::-1]]]


def ring_reduce(blocks):
    half = blocks[4].shape[0] // 2
    low, high = shift(blocks[4][:half], "z", -1), shift(blocks[4][half:], "z", 1)
    left = blocks[3] + jnp.concatenate([low, jnp.zeros_like(low)], axis=0)
    right = blocks[5] + jnp.concatenate([jnp.zeros_like(high), high], axis=0)
    for near in (2, 1):
        left = blocks[near] + shift(left, "z", -1)
        right = blocks[8 - near] + shift(right, "z", 1)
    f32 = jnp.float32
    return (
        blocks[0].astype(f32)
        + shift(left, "z", -1).astype(f32)
        + shift(right, "z", 1).astype(f32)
    )


def plane_gather(x):
    rows = x.shape[0]
    pair = jnp.concatenate([x, flip(x, "xl")], axis=0)
    left, right = shift(pair, "y", 1), shift(pair, "y", -1)
    low, high = shift(left[:rows], "y", 1), shift(right[rows:], "y", -1)
    return [pair, left, low, high, right]


def fill(target, refs):
    row = 0
    for ref in refs:
        count = ref.shape[0]
        target[row : row + count, :] = ref[...]
        row += count


def owner_of(index_ref, place):
    return lax.rem(index_ref[0] + 8 - place, 8)


def key_owner_of(index_ref, place):
    d, a = divmod(place, 2)
    return 4 * lax.rem(index_ref[2] + a, 2) + lax.rem(index_ref[1] + 4 - d, 4)


def split(refs, counts):
    out, first = [], 0
    for count in counts:
        out.append(refs[first : first + count])
        first += count
    return out, refs[first:]


def stats_kernel(places, counts, heads, index_ref, *refs):
    sides, (stats_ref, *scratch) = split(refs, counts)
    for target, side in zip(scratch, sides):
        fill(target, side)
    q_ref, c_ref, k_ref, v_ref = scratch
    h = pl.program_id(0)
    for t in range(0, len(places), 2):
        cols = slice(t * 128, t * 128 + 256)
        s = lax.dot_general(k_ref[...], q_ref[cols, :], NT, preferred_element_type=jnp.float32)
        g = lax.dot_general(v_ref[...], c_ref[cols, :], NT, preferred_element_type=jnp.float32)
        s = s * (SCALING * LOG2E)
        top = jnp.max(s, axis=0, keepdims=True)
        e = jnp.exp2(s - top)
        total = jnp.sum(e, axis=0, keepdims=True)
        weight = jnp.sum(e * g, axis=0, keepdims=True)
        for side in (0, 1):
            owner = owner_of(index_ref, places[t + side])
            part = slice(side * 128, side * 128 + 128)
            for kind, row in enumerate((top, total, weight)):
                stats_ref[owner, pl.ds(heads * kind + h, 1), :] = row[:, part]


def grads_kernel(places, counts, heads, index_ref, *refs):
    sides, (totals_ref, *rest) = split(refs, counts)
    dq_refs, dkv_ref, scratch, (dk_ref, dv_ref) = rest[:8], rest[8], rest[9:13], rest[13:]
    for target, side in zip(scratch, sides):
        fill(target, side)
    q_ref, c_ref, k_ref, v_ref = scratch
    k_turned = k_ref[...].astype(jnp.float32).T.astype(jnp.bfloat16)
    h = pl.program_id(0)
    for t in range(0, len(places), 2):
        cols = slice(t * 128, t * 128 + 256)
        owners = [owner_of(index_ref, place) for place in places[t : t + 2]]
        log_total, delta = (
            jnp.concatenate(
                [totals_ref[owner, pl.ds(heads * kind + h, 1), :] for owner in owners], axis=1
            )
            for kind in (0, 1)
        )
        s = lax.dot_general(k_ref[...], q_ref[cols, :], NT, preferred_element_type=jnp.float32)
        g = lax.dot_general(v_ref[...], c_ref[cols, :], NT, preferred_element_type=jnp.float32)
        p = jnp.exp2(s * (SCALING * LOG2E) - log_total)
        ds = (p * (g - delta)).astype(jnp.bfloat16)
        dv = jnp.dot(p.astype(jnp.bfloat16), c_ref[cols, :], preferred_element_type=jnp.float32)
        dk = jnp.dot(ds, q_ref[cols, :], preferred_element_type=jnp.float32)
        if t == 0:
            dv_ref[...] = dv
            dk_ref[...] = dk
        else:
            dv_ref[...] += dv
            dk_ref[...] += dk
        dq = jnp.dot(k_turned, ds, preferred_element_type=jnp.float32)
        dq = (dq * SCALING).T.astype(jnp.bfloat16)
        dq_refs[t][...] = dq[:128]
        dq_refs[t + 1][...] = dq[128:]
    for place in range(8):
        owner = key_owner_of(index_ref, place)
        rows = slice(place * 128, place * 128 + 128)
        dkv_ref[owner, 0] = (dk_ref[rows, :] * SCALING).astype(jnp.bfloat16)
        dkv_ref[owner, 1] = dv_ref[rows, :].astype(jnp.bfloat16)


SMEM_SPEC = pl.BlockSpec(memory_space=pltpu.SMEM)
ROWS_SPEC = pl.BlockSpec((8, 16, 128), lambda h: (0, 0, 0))


def side_specs(pieces, first):
    return [
        pl.BlockSpec((piece.shape[0], HEAD_DIM), lambda h: (0, first + h)) for piece in pieces
    ]


def sides_of(blocks, keys, heads):
    pieces = [piece for block in blocks for piece in block]
    operands = [*pieces, *pieces, *keys, *keys]
    specs = []
    for side in (pieces, keys):
        for first in (0, heads):
            specs += side_specs(side, first)
    return operands, specs, [len(pieces)] * 2 + [len(keys)] * 2


def block_stats(index, places, blocks, keys, heads):
    operands, specs, counts = sides_of(blocks, keys, heads)
    rows = 128 * len(blocks)
    return pl.pallas_call(
        functools.partial(stats_kernel, places, counts, heads),
        grid=(heads,),
        out_shape=jax.ShapeDtypeStruct((8, 16, 128), jnp.float32),
        in_specs=[SMEM_SPEC, *specs],
        out_specs=ROWS_SPEC,
        scratch_shapes=[pltpu.VMEM((rows, HEAD_DIM), jnp.bfloat16)] * 2
        + [pltpu.VMEM((1024, HEAD_DIM), jnp.bfloat16)] * 2,
        compiler_params=pltpu.CompilerParams(vmem_limit_bytes=VMEM_LIMIT),
        cost_estimate=pl.CostEstimate(
            flops=heads * rows * 2**17 * 16, bytes_accessed=2**23, transcendentals=heads * rows * 2**10
        ),
        name="block_stats",
    )(index, *operands)


def block_grads(index, places, blocks, keys, totals, heads):
    operands, specs, counts = sides_of(blocks, keys, heads)
    rows = 128 * len(blocks)
    width = heads * HEAD_DIM
    outs = pl.pallas_call(
        functools.partial(grads_kernel, places, counts, heads),
        grid=(heads,),
        out_shape=[jax.ShapeDtypeStruct((128, width), jnp.bfloat16)] * 8
        + [jax.ShapeDtypeStruct((8, 2, 128, width), jnp.bfloat16)],
        in_specs=[SMEM_SPEC, *specs, ROWS_SPEC],
        out_specs=[pl.BlockSpec((128, HEAD_DIM), lambda h: (0, h))] * 8
        + [pl.BlockSpec((8, 2, 128, HEAD_DIM), lambda h: (0, 0, 0, h))],
        scratch_shapes=[pltpu.VMEM((rows, HEAD_DIM), jnp.bfloat16)] * 2
        + [pltpu.VMEM((1024, HEAD_DIM), jnp.bfloat16)] * 2
        + [pltpu.VMEM((1024, HEAD_DIM), jnp.float32)] * 2,
        compiler_params=pltpu.CompilerParams(vmem_limit_bytes=VMEM_LIMIT),
        cost_estimate=pl.CostEstimate(
            flops=heads * rows * 2**17 * 20, bytes_accessed=2**24, transcendentals=heads * rows * 2**10
        ),
        name="block_grads",
    )(index, *operands, totals)
    return outs[:8], outs[8]


def merge(parts, heads):
    kinds = [
        [part[:, first * heads : (first + 1) * heads] for first in range(3)] for part in parts
    ]
    top = functools.reduce(jnp.maximum, [kind[0] for kind in kinds])
    total = weight = 0.0
    for kind in kinds:
        factor = jnp.exp2(kind[0] - top)
        total = total + kind[1] * factor
        weight = weight + kind[2] * factor
    return top, total, weight


def with_padding(rows):
    used = sum(row.shape[1] for row in rows)
    return jnp.concatenate([*rows, jnp.zeros((8, 16 - used, 128), jnp.float32)], axis=1)


def shards(q_raw, k_raw, values, positions, cotangent, out_weight, modulation, step_index):
    width = q_raw.shape[1]
    heads = width // HEAD_DIM
    inner_width = width * 4
    f32 = jnp.float32
    q_float = q_raw.astype(f32)
    k_float = k_raw.astype(f32)
    squares = jnp.stack(
        [jnp.sum(q_float * q_float, axis=1), jnp.sum(k_float * k_float, axis=1)]
    )
    inverse = lax.rsqrt(sum_heads_axes(squares) / inner_width + EPSILON)
    cosine, signed_sine = rotation(positions, heads)
    q_normed = q_float * inverse[0][:, None]
    k_normed = k_float * inverse[1][:, None]
    q_rot = rotate(q_normed, cosine, signed_sine, 1.0).astype(jnp.bfloat16)
    k_rot = rotate(k_normed, cosine, signed_sine, 1.0).astype(jnp.bfloat16)
    gate_row = lax.dynamic_slice_in_dim(modulation, step_index[0], 1, 0)
    gated_cot = (gate_row * cotangent.astype(f32)).astype(jnp.bfloat16)
    attn_cot = lax.dot_general(
        gated_cot, out_weight, NT, preferred_element_type=f32
    ).astype(jnp.bfloat16)

    index = jnp.stack([lax.axis_index("z"), lax.axis_index("y"), lax.axis_index("xl")])
    queries = ring_gather(jnp.concatenate([q_rot, attn_cot], axis=1))
    keys = plane_gather(jnp.concatenate([k_rot, values], axis=1))

    places = list(range(8))
    stats = block_stats(index, places, queries, keys, heads)
    stats = with_padding(merge([stats, shift(stats, "z", 1)], heads))
    top, total, weight = merge([stats] + [shift(stats, "z", d) for d in (2, -2, 4)], heads)
    totals = with_padding([top + jnp.log2(total), weight / total])

    dq, dkv = block_grads(index, places, queries, keys, totals, heads)
    dq_sum = ring_reduce(dq)
    dkv_sum = jnp.sum(lax.all_to_all(dkv, ("xl", "y"), 0, 0, tiled=True).astype(f32), axis=0)

    dq_normed = rotate(dq_sum, cosine, signed_sine, -1.0)
    dk_normed = rotate(dkv_sum[0], cosine, signed_sine, -1.0)
    slopes = jnp.stack(
        [jnp.sum(dq_normed * q_normed, axis=1), jnp.sum(dk_normed * k_normed, axis=1)]
    )
    slopes = sum_heads_axes(slopes) / inner_width
    query_grad = inverse[0][:, None] * (dq_normed - q_normed * slopes[0][:, None])
    key_grad = inverse[1][:, None] * (dk_normed - k_normed * slopes[1][:, None])
    return (
        query_grad.astype(jnp.bfloat16),
        key_grad.astype(jnp.bfloat16),
        dkv_sum[1].astype(jnp.bfloat16),
    )


def solution(mesh):
    axes = ("xl", "z", "y", "xh", "c")
    fine = Mesh(np.asarray(mesh.devices).reshape(2, 8, 4, 2, 2), axes)
    split = P(TOKENS_AXES, HEADS_AXES)
    rows = P(TOKENS_AXES, None)
    return jax.shard_map(
        shards,
        mesh=fine,
        in_specs=(split, split, split, rows, rows, P(HEADS_AXES, None), P(), P()),
        out_specs=(split, split, split),
        check_vma=False,
    )
```

```python
import functools
import math

import jax
import jax.numpy as jnp
import numpy as np
from jax import lax
from jax.experimental import pallas as pl
from jax.experimental.pallas import tpu as pltpu
from jax.sharding import Mesh
from jax.sharding import PartitionSpec as P

HEAD_DIM = 128
EPSILON = 1e-06
LOG2E = math.log2(math.e)
SCALING = 1.0 / math.sqrt(HEAD_DIM)
TOKENS_AXES = ("xl", "z", "y")
HEADS_AXES = ("xh", "c")
VMEM_LIMIT = 58 * 1024 * 1024
NT = (((1,), (1,)), ((), ()))
TN = (((0,), (0,)), ((), ()))


def angle_table(head_size):
    side_dim = 2 * (head_size // 6)
    first_dim = head_size - 2 * side_dim
    freq_table = np.zeros((3, head_size // 2), np.float32)
    column = 0
    for axis_number, group_dim in enumerate([first_dim, side_dim, side_dim]):
        for pair_index in range(group_dim // 2):
            freq_table[axis_number, column] = 10000.0 ** (-2.0 * pair_index / group_dim)
            column += 1
    return freq_table


def rotation(positions, heads_count):
    table = np.repeat(angle_table(HEAD_DIM), 2, axis=1)
    place = positions.astype(jnp.float32)
    angles = sum(place[:, axis : axis + 1] * jnp.asarray(table[axis])[None, :] for axis in range(3))
    parity = jnp.asarray(np.tile(np.array([-1.0, 1.0], np.float32), HEAD_DIM // 2))
    cosine, signed_sine = lax.optimization_barrier(
        (jnp.cos(angles), jnp.sin(angles) * parity[None, :])
    )
    return (
        jnp.concatenate([cosine] * heads_count, axis=1),
        jnp.concatenate([signed_sine] * heads_count, axis=1),
    )


def partner_of(source):
    columns = np.arange(source.shape[1])
    exchange = (columns[:, None] == (columns ^ 1)[None, :]).astype(np.float32)
    return jnp.dot(
        source, jnp.asarray(exchange, dtype=jnp.bfloat16), preferred_element_type=jnp.float32
    )


def rotate(source, cosine, signed_sine, direction):
    column_ids = jnp.arange(source.shape[1])
    partner = jnp.where(
        column_ids % 2 == 0, jnp.roll(source, -1, axis=1), jnp.roll(source, 1, axis=1)
    )
    return source * cosine + direction * partner * signed_sine


def shift(x, axis, distance):
    size = lax.axis_size(axis)
    return lax.ppermute(x, axis, [(i, (i + distance) % size) for i in range(size)])


def flip(x, axis):
    return lax.ppermute(x, axis, [(0, 1), (1, 0)])


def sum_heads_axes(x):
    total = x
    for mask in (1, 2, 3):
        total = total + lax.ppermute(x, HEADS_AXES, [(i, i ^ mask) for i in range(4)])
    return total


def ring_gather(x):
    half = x.shape[0] // 2
    left, right = x, x
    from_left, from_right = [], []
    for _ in range(3):
        left, right = shift(left, "z", 1), shift(right, "z", -1)
        from_left.append(left)
        from_right.append(right)
    far = [shift(left[:half], "z", 1), shift(right[half:], "z", -1)]
    return [[x], *[[b] for b in from_left], far, *[[b] for b in from_right[::-1]]]


def ring_reduce(blocks):
    half = blocks[4].shape[0] // 2
    low, high = shift(blocks[4][:half], "z", -1), shift(blocks[4][half:], "z", 1)
    left = blocks[3] + jnp.concatenate([low, jnp.zeros_like(low)], axis=0)
    right = blocks[5] + jnp.concatenate([jnp.zeros_like(high), high], axis=0)
    for near in (2, 1):
        left = blocks[near] + shift(left, "z", -1)
        right = blocks[8 - near] + shift(right, "z", 1)
    f32 = jnp.float32
    return (
        blocks[0].astype(f32)
        + shift(left, "z", -1).astype(f32)
        + shift(right, "z", 1).astype(f32)
    )


def plane_gather(x):
    rows = x.shape[0]
    pair = jnp.concatenate([x, flip(x, "xl")], axis=0)
    left, right = shift(pair, "y", 1), shift(pair, "y", -1)
    low, high = shift(left[:rows], "y", 1), shift(right[rows:], "y", -1)
    return [pair, left, low, high, right]


def fill(target, refs):
    row = 0
    for ref in refs:
        count = ref.shape[0]
        target[row : row + count, :] = ref[...]
        row += count


def owner_of(index_ref, place):
    return lax.rem(index_ref[0] + 8 - place, 8)


def key_owner_of(index_ref, place):
    d, a = divmod(place, 2)
    return 4 * lax.rem(index_ref[2] + a, 2) + lax.rem(index_ref[1] + 4 - d, 4)


def split(refs, counts):
    out, first = [], 0
    for count in counts:
        out.append(refs[first : first + count])
        first += count
    return out, refs[first:]


def stats_kernel(places, counts, heads, index_ref, *refs):
    sides, (stats_ref, *scratch) = split(refs, counts)
    for target, side in zip(scratch, sides):
        fill(target, side)
    q_ref, c_ref, k_ref, v_ref = scratch
    h = pl.program_id(0)
    for t in range(0, len(places), 4):
        cols = slice(t * 128, t * 128 + 512)
        s = lax.dot_general(k_ref[...], q_ref[cols, :], NT, preferred_element_type=jnp.float32)
        g = lax.dot_general(v_ref[...], c_ref[cols, :], NT, preferred_element_type=jnp.float32)
        top = jnp.max(s, axis=0, keepdims=True)
        e = jnp.exp2(s - top)
        total = jnp.sum(e, axis=0, keepdims=True)
        weight = jnp.sum(e * g, axis=0, keepdims=True)
        for side in range(4):
            owner = owner_of(index_ref, places[t + side])
            part = slice(side * 128, side * 128 + 128)
            for kind, row in enumerate((top, total, weight)):
                stats_ref[owner, pl.ds(heads * kind + h, 1), :] = row[:, part]


def grads_kernel(places, counts, heads, index_ref, *refs):
    sides, (totals_ref, *rest) = split(refs, counts)
    dq_refs, dkv_ref, scratch, (dk_ref, dv_ref) = rest[:8], rest[8], rest[9:13], rest[13:]
    for target, side in zip(scratch, sides):
        fill(target, side)
    q_ref, c_ref, k_ref, v_ref = scratch
    k_turned = k_ref[...].astype(jnp.float32).T.astype(jnp.bfloat16)
    h = pl.program_id(0)
    for t in range(0, len(places), 2):
        cols = slice(t * 128, t * 128 + 256)
        owners = [owner_of(index_ref, place) for place in places[t : t + 2]]
        log_total, delta = (
            jnp.concatenate(
                [totals_ref[owner, pl.ds(heads * kind + h, 1), :] for owner in owners], axis=1
            )
            for kind in (0, 1)
        )
        s = lax.dot_general(k_ref[...], q_ref[cols, :], NT, preferred_element_type=jnp.float32)
        g = lax.dot_general(v_ref[...], c_ref[cols, :], NT, preferred_element_type=jnp.float32)
        p = jnp.exp2(s - log_total)
        ds = (p * (g - delta)).astype(jnp.bfloat16)
        dv = jnp.dot(p.astype(jnp.bfloat16), c_ref[cols, :], preferred_element_type=jnp.float32)
        dk = jnp.dot(ds, q_ref[cols, :], preferred_element_type=jnp.float32)
        if t == 0:
            dv_ref[...] = dv
            dk_ref[...] = dk
        else:
            dv_ref[...] += dv
            dk_ref[...] += dk
        dq = jnp.dot(k_turned, ds, preferred_element_type=jnp.float32)
        dq = (dq / LOG2E).T.astype(jnp.bfloat16)
        dq_refs[t][...] = dq[:128]
        dq_refs[t + 1][...] = dq[128:]
    for place in range(8):
        owner = key_owner_of(index_ref, place)
        rows = slice(place * 128, place * 128 + 128)
        dkv_ref[owner, 0] = (dk_ref[rows, :] * SCALING).astype(jnp.bfloat16)
        dkv_ref[owner, 1] = dv_ref[rows, :].astype(jnp.bfloat16)


SMEM_SPEC = pl.BlockSpec(memory_space=pltpu.SMEM)
ROWS_SPEC = pl.BlockSpec((8, 16, 128), lambda h: (0, 0, 0))


def side_specs(pieces, first):
    return [
        pl.BlockSpec((piece.shape[0], HEAD_DIM), lambda h: (0, first + h)) for piece in pieces
    ]


def sides_of(blocks, keys, heads):
    pieces = [piece for block in blocks for piece in block]
    operands = [*pieces, *pieces, *keys, *keys]
    specs = []
    for side in (pieces, keys):
        for first in (0, heads):
            specs += side_specs(side, first)
    return operands, specs, [len(pieces)] * 2 + [len(keys)] * 2


def block_stats(index, places, blocks, keys, heads):
    operands, specs, counts = sides_of(blocks, keys, heads)
    rows = 128 * len(blocks)
    return pl.pallas_call(
        functools.partial(stats_kernel, places, counts, heads),
        grid=(heads,),
        out_shape=jax.ShapeDtypeStruct((8, 16, 128), jnp.float32),
        in_specs=[SMEM_SPEC, *specs],
        out_specs=ROWS_SPEC,
        scratch_shapes=[pltpu.VMEM((rows, HEAD_DIM), jnp.bfloat16)] * 2
        + [pltpu.VMEM((1024, HEAD_DIM), jnp.bfloat16)] * 2,
        compiler_params=pltpu.CompilerParams(vmem_limit_bytes=VMEM_LIMIT),
        cost_estimate=pl.CostEstimate(
            flops=heads * rows * 2**17 * 16, bytes_accessed=2**23, transcendentals=heads * rows * 2**10
        ),
        name="block_stats",
    )(index, *operands)


def block_grads(index, places, blocks, keys, totals, heads):
    operands, specs, counts = sides_of(blocks, keys, heads)
    rows = 128 * len(blocks)
    width = heads * HEAD_DIM
    outs = pl.pallas_call(
        functools.partial(grads_kernel, places, counts, heads),
        grid=(heads,),
        out_shape=[jax.ShapeDtypeStruct((128, width), jnp.bfloat16)] * 8
        + [jax.ShapeDtypeStruct((8, 2, 128, width), jnp.bfloat16)],
        in_specs=[SMEM_SPEC, *specs, ROWS_SPEC],
        out_specs=[pl.BlockSpec((128, HEAD_DIM), lambda h: (0, h))] * 8
        + [pl.BlockSpec((8, 2, 128, HEAD_DIM), lambda h: (0, 0, 0, h))],
        scratch_shapes=[pltpu.VMEM((rows, HEAD_DIM), jnp.bfloat16)] * 2
        + [pltpu.VMEM((1024, HEAD_DIM), jnp.bfloat16)] * 2
        + [pltpu.VMEM((1024, HEAD_DIM), jnp.float32)] * 2,
        compiler_params=pltpu.CompilerParams(vmem_limit_bytes=VMEM_LIMIT),
        cost_estimate=pl.CostEstimate(
            flops=heads * rows * 2**17 * 20, bytes_accessed=2**24, transcendentals=heads * rows * 2**10
        ),
        name="block_grads",
    )(index, *operands, totals)
    return outs[:8], outs[8]


def merge(parts, heads):
    kinds = [
        [part[:, first * heads : (first + 1) * heads] for first in range(3)] for part in parts
    ]
    top = functools.reduce(jnp.maximum, [kind[0] for kind in kinds])
    total = weight = 0.0
    for kind in kinds:
        factor = jnp.exp2(kind[0] - top)
        total = total + kind[1] * factor
        weight = weight + kind[2] * factor
    return top, total, weight


def with_padding(rows):
    used = sum(row.shape[1] for row in rows)
    return jnp.concatenate([*rows, jnp.zeros((8, 16 - used, 128), jnp.float32)], axis=1)


def shards(q_raw, k_raw, values, positions, cotangent, out_weight, modulation, step_index):
    width = q_raw.shape[1]
    heads = width // HEAD_DIM
    inner_width = width * 4
    f32 = jnp.float32
    q_float = q_raw.astype(f32)
    k_float = k_raw.astype(f32)
    both = jnp.stack([q_raw, k_raw]).astype(f32)
    squares = jnp.sum(both * both, axis=2)
    cosine, signed_sine = rotation(positions, heads)
    squares = squares + flip(squares, "c")
    squares, cotangent = lax.optimization_barrier((squares, cotangent))
    inverse = lax.rsqrt((squares + flip(squares, "xh")) / inner_width + EPSILON)
    q_normed = q_float * inverse[0][:, None]
    k_normed = k_float * inverse[1][:, None]
    q_rot, k_rot = (
        (
            (factor * inverse[row])[:, None]
            * (raw.astype(f32) * cosine + partner_of(raw) * signed_sine)
        ).astype(jnp.bfloat16)
        for row, (raw, factor) in enumerate(((q_raw, 1.0), (k_raw, SCALING * LOG2E)))
    )
    gate_row = lax.dynamic_slice_in_dim(modulation, step_index[0], 1, 0)
    gated_cot = (gate_row * cotangent.astype(f32)).astype(jnp.bfloat16)
    attn_cot = lax.dot_general(
        gated_cot, out_weight, NT, preferred_element_type=f32
    ).astype(jnp.bfloat16)

    index = jnp.stack([lax.axis_index("z"), lax.axis_index("y"), lax.axis_index("xl")])
    queries = ring_gather(jnp.concatenate([q_rot, attn_cot], axis=1))
    keys = plane_gather(jnp.concatenate([k_rot, values], axis=1))

    places = list(range(8))
    stats = block_stats(index, places, queries, keys, heads)
    stats = with_padding(merge([stats, shift(stats, "z", 1)], heads))
    top, total, weight = merge([stats] + [shift(stats, "z", d) for d in (2, -2, 4)], heads)
    totals = with_padding([top + jnp.log2(total), weight / total])

    dq, dkv = block_grads(index, places, queries, keys, totals, heads)
    dq_sum = ring_reduce(dq)
    dkv_sum = jnp.sum(lax.all_to_all(dkv, ("xl", "y"), 0, 0, tiled=True).astype(f32), axis=0)

    dq_normed = rotate(dq_sum, cosine, signed_sine, -1.0)
    dk_normed = rotate(dkv_sum[0], cosine, signed_sine, -1.0)
    slopes = jnp.stack(
        [jnp.sum(dq_normed * q_normed, axis=1), jnp.sum(dk_normed * k_normed, axis=1)]
    )
    slopes = sum_heads_axes(slopes) / inner_width
    query_grad = inverse[0][:, None] * (dq_normed - q_normed * slopes[0][:, None])
    key_grad = inverse[1][:, None] * (dk_normed - k_normed * slopes[1][:, None])
    return (
        query_grad.astype(jnp.bfloat16),
        key_grad.astype(jnp.bfloat16),
        dkv_sum[1].astype(jnp.bfloat16),
    )


def solution(mesh):
    axes = ("xl", "z", "y", "xh", "c")
    fine = Mesh(np.asarray(mesh.devices).reshape(2, 8, 4, 2, 2), axes)
    split = P(TOKENS_AXES, HEADS_AXES)
    rows = P(TOKENS_AXES, None)
    return jax.shard_map(
        shards,
        mesh=fine,
        in_specs=(split, split, split, rows, rows, P(HEADS_AXES, None), P(), P()),
        out_specs=(split, split, split),
        check_vma=False,
    )
```

```python
import functools
import math

import jax
import jax.numpy as jnp
import numpy as np
from jax import lax
from jax.experimental import pallas as pl
from jax.experimental.pallas import tpu as pltpu
from jax.sharding import Mesh
from jax.sharding import PartitionSpec as P

HEAD_DIM = 128
EPSILON = 1e-06
LOG2E = math.log2(math.e)
SCALING = 1.0 / math.sqrt(HEAD_DIM)
TOKENS_AXES = ("xl", "z", "y")
HEADS_AXES = ("xh", "c")
VMEM_LIMIT = 58 * 1024 * 1024
NT = (((1,), (1,)), ((), ()))
TN = (((0,), (0,)), ((), ()))


def angle_table(head_size):
    side_dim = 2 * (head_size // 6)
    first_dim = head_size - 2 * side_dim
    freq_table = np.zeros((3, head_size // 2), np.float32)
    column = 0
    for axis_number, group_dim in enumerate([first_dim, side_dim, side_dim]):
        for pair_index in range(group_dim // 2):
            freq_table[axis_number, column] = 10000.0 ** (-2.0 * pair_index / group_dim)
            column += 1
    return freq_table


def rotation(positions, heads_count):
    table = np.repeat(angle_table(HEAD_DIM), 2, axis=1)
    place = positions.astype(jnp.float32)
    angles = sum(place[:, axis : axis + 1] * jnp.asarray(table[axis])[None, :] for axis in range(3))
    parity = jnp.asarray(np.tile(np.array([-1.0, 1.0], np.float32), HEAD_DIM // 2))
    cosine, signed_sine = lax.optimization_barrier(
        (jnp.cos(angles), jnp.sin(angles) * parity[None, :])
    )
    return (
        jnp.concatenate([cosine] * heads_count, axis=1),
        jnp.concatenate([signed_sine] * heads_count, axis=1),
    )


def partner_of(source):
    columns = np.arange(source.shape[1])
    exchange = (columns[:, None] == (columns ^ 1)[None, :]).astype(np.float32)
    return jnp.dot(
        source, jnp.asarray(exchange, dtype=jnp.bfloat16), preferred_element_type=jnp.float32
    )


def rotate(source, cosine, signed_sine, direction):
    column_ids = jnp.arange(source.shape[1])
    partner = jnp.where(
        column_ids % 2 == 0, jnp.roll(source, -1, axis=1), jnp.roll(source, 1, axis=1)
    )
    return source * cosine + direction * partner * signed_sine


def shift(x, axis, distance):
    size = lax.axis_size(axis)
    return lax.ppermute(x, axis, [(i, (i + distance) % size) for i in range(size)])


def swap(x, axis, mask):
    return lax.ppermute(x, axis, [(i, i ^ mask) for i in range(lax.axis_size(axis))])


def flip(x, axis):
    return lax.ppermute(x, axis, [(0, 1), (1, 0)])


def sum_heads_axes(x):
    total = x
    for mask in (1, 2, 3):
        total = total + lax.ppermute(x, HEADS_AXES, [(i, i ^ mask) for i in range(4)])
    return total


def ring_gather(x):
    half = x.shape[0] // 2
    left, right = x, x
    from_left, from_right = [], []
    for _ in range(3):
        left, right = shift(left, "z", 1), shift(right, "z", -1)
        from_left.append(left)
        from_right.append(right)
    far = [shift(left[:half], "z", 1), shift(right[half:], "z", -1)]
    return [[x], *[[b] for b in from_left], far, *[[b] for b in from_right[::-1]]]


def ring_reduce(blocks):
    half = blocks[4].shape[0] // 2
    low, high = shift(blocks[4][:half], "z", -2), shift(blocks[4][half:], "z", 2)
    left = (
        blocks[2]
        + shift(blocks[3], "z", -1)
        + jnp.concatenate([low, jnp.zeros_like(low)], axis=0)
    )
    right = (
        blocks[6]
        + shift(blocks[5], "z", 1)
        + jnp.concatenate([jnp.zeros_like(high), high], axis=0)
    )
    left = blocks[1] + shift(left, "z", -1)
    right = blocks[7] + shift(right, "z", 1)
    f32 = jnp.float32
    return (
        blocks[0].astype(f32)
        + shift(left, "z", -1).astype(f32)
        + shift(right, "z", 1).astype(f32)
    )


def plane_gather(x, flipped):
    rows = x.shape[0]
    pair = jnp.concatenate([x, flipped], axis=0)
    left, right = shift(pair, "y", 1), shift(pair, "y", -1)
    low, high = shift(left[:rows], "y", 1), shift(right[rows:], "y", -1)
    return [pair, left, low, high, right]


def fill(target, refs):
    row = 0
    for ref in refs:
        count = ref.shape[0]
        target[row : row + count, :] = ref[...]
        row += count


def owner_of(index_ref, place):
    return lax.rem(index_ref[0] + 8 - place, 8)


def key_owner_of(index_ref, place):
    d, a = divmod(place, 2)
    return 4 * lax.rem(index_ref[2] + a, 2) + lax.rem(index_ref[1] + 4 - d, 4)


def split(refs, counts):
    out, first = [], 0
    for count in counts:
        out.append(refs[first : first + count])
        first += count
    return out, refs[first:]


def stats_kernel(places, counts, heads, index_ref, *refs):
    sides, (stats_ref, *scratch) = split(refs, counts)
    for target, side in zip(scratch, sides):
        fill(target, side)
    q_ref, c_ref, k_ref, v_ref = scratch
    h = pl.program_id(0)
    for t in range(0, len(places), 4):
        cols = slice(t * 128, t * 128 + 512)
        s = lax.dot_general(k_ref[...], q_ref[cols, :], NT, preferred_element_type=jnp.float32)
        g = lax.dot_general(v_ref[...], c_ref[cols, :], NT, preferred_element_type=jnp.float32)
        top = jnp.max(s, axis=0, keepdims=True)
        e = jnp.exp2(s - top)
        total = jnp.sum(e, axis=0, keepdims=True)
        weight = jnp.sum(e * g, axis=0, keepdims=True)
        for side in range(4):
            owner = owner_of(index_ref, places[t + side])
            part = slice(side * 128, side * 128 + 128)
            for kind, row in enumerate((top, total, weight)):
                stats_ref[owner, pl.ds(heads * kind + h, 1), :] = row[:, part]


def grads_kernel(places, counts, heads, index_ref, *refs):
    sides, (totals_ref, *rest) = split(refs, counts)
    dq_refs, dkv_ref, scratch, (dk_ref, dv_ref) = rest[:8], rest[8], rest[9:13], rest[13:]
    for target, side in zip(scratch, sides):
        fill(target, side)
    q_ref, c_ref, k_ref, v_ref = scratch
    k_turned = k_ref[...].astype(jnp.float32).T.astype(jnp.bfloat16)
    h = pl.program_id(0)
    for t in range(0, len(places), 2):
        cols = slice(t * 128, t * 128 + 256)
        owners = [owner_of(index_ref, place) for place in places[t : t + 2]]
        log_total, delta = (
            jnp.concatenate(
                [totals_ref[owner, pl.ds(heads * kind + h, 1), :] for owner in owners], axis=1
            )
            for kind in (0, 1)
        )
        s = lax.dot_general(k_ref[...], q_ref[cols, :], NT, preferred_element_type=jnp.float32)
        g = lax.dot_general(v_ref[...], c_ref[cols, :], NT, preferred_element_type=jnp.float32)
        p = jnp.exp2(s - log_total)
        ds = (p * (g - delta)).astype(jnp.bfloat16)
        dv = jnp.dot(p.astype(jnp.bfloat16), c_ref[cols, :], preferred_element_type=jnp.float32)
        dk = jnp.dot(ds, q_ref[cols, :], preferred_element_type=jnp.float32)
        if t == 0:
            dv_ref[...] = dv
            dk_ref[...] = dk
        else:
            dv_ref[...] += dv
            dk_ref[...] += dk
        dq = jnp.dot(k_turned, ds, preferred_element_type=jnp.float32)
        dq = (dq / LOG2E).T.astype(jnp.bfloat16)
        dq_refs[t][...] = dq[:128]
        dq_refs[t + 1][...] = dq[128:]
    for place in range(8):
        owner = key_owner_of(index_ref, place)
        rows = slice(place * 128, place * 128 + 128)
        dkv_ref[owner, 0] = (dk_ref[rows, :] * SCALING).astype(jnp.bfloat16)
        dkv_ref[owner, 1] = dv_ref[rows, :].astype(jnp.bfloat16)


SMEM_SPEC = pl.BlockSpec(memory_space=pltpu.SMEM)
ROWS_SPEC = pl.BlockSpec((8, 16, 128), lambda h: (0, 0, 0))


def side_specs(pieces, first):
    return [
        pl.BlockSpec((piece.shape[0], HEAD_DIM), lambda h: (0, first + h)) for piece in pieces
    ]


def sides_of(blocks, keys, heads):
    pieces = [piece for block in blocks for piece in block]
    operands = [*pieces, *pieces, *keys, *keys]
    specs = []
    for side in (pieces, keys):
        for first in (0, heads):
            specs += side_specs(side, first)
    return operands, specs, [len(pieces)] * 2 + [len(keys)] * 2


def block_stats(index, places, blocks, keys, heads):
    operands, specs, counts = sides_of(blocks, keys, heads)
    rows = 128 * len(blocks)
    return pl.pallas_call(
        functools.partial(stats_kernel, places, counts, heads),
        grid=(heads,),
        out_shape=jax.ShapeDtypeStruct((8, 16, 128), jnp.float32),
        in_specs=[SMEM_SPEC, *specs],
        out_specs=ROWS_SPEC,
        scratch_shapes=[pltpu.VMEM((rows, HEAD_DIM), jnp.bfloat16)] * 2
        + [pltpu.VMEM((1024, HEAD_DIM), jnp.bfloat16)] * 2,
        compiler_params=pltpu.CompilerParams(vmem_limit_bytes=VMEM_LIMIT),
        cost_estimate=pl.CostEstimate(
            flops=heads * rows * 2**17 * 16, bytes_accessed=2**23, transcendentals=heads * rows * 2**10
        ),
        name="block_stats",
    )(index, *operands)


def block_grads(index, places, blocks, keys, totals, heads):
    operands, specs, counts = sides_of(blocks, keys, heads)
    rows = 128 * len(blocks)
    width = heads * HEAD_DIM
    outs = pl.pallas_call(
        functools.partial(grads_kernel, places, counts, heads),
        grid=(heads,),
        out_shape=[jax.ShapeDtypeStruct((128, width), jnp.bfloat16)] * 8
        + [jax.ShapeDtypeStruct((8, 2, 128, width), jnp.bfloat16)],
        in_specs=[SMEM_SPEC, *specs, ROWS_SPEC],
        out_specs=[pl.BlockSpec((128, HEAD_DIM), lambda h: (0, h))] * 8
        + [pl.BlockSpec((8, 2, 128, HEAD_DIM), lambda h: (0, 0, 0, h))],
        scratch_shapes=[pltpu.VMEM((rows, HEAD_DIM), jnp.bfloat16)] * 2
        + [pltpu.VMEM((1024, HEAD_DIM), jnp.bfloat16)] * 2
        + [pltpu.VMEM((1024, HEAD_DIM), jnp.float32)] * 2,
        compiler_params=pltpu.CompilerParams(vmem_limit_bytes=VMEM_LIMIT),
        cost_estimate=pl.CostEstimate(
            flops=heads * rows * 2**17 * 20, bytes_accessed=2**24, transcendentals=heads * rows * 2**10
        ),
        name="block_grads",
    )(index, *operands, totals)
    return outs[:8], outs[8]


def merge(parts, heads):
    tops = [
        jnp.concatenate([part[:, :heads]] * 3 + [part[:, : 16 - 3 * heads]], axis=1)
        for part in parts
    ]
    top = functools.reduce(jnp.maximum, tops)
    total = sum(part * jnp.exp2(own - top) for part, own in zip(parts, tops))
    return jnp.where(jnp.arange(16)[None, :, None] < heads, top, total)


def shards(q_raw, k_raw, values, positions, cotangent, out_weight, modulation, step_index):
    width = q_raw.shape[1]
    heads = width // HEAD_DIM
    inner_width = width * 4
    f32 = jnp.float32
    q_float = q_raw.astype(f32)
    k_float = k_raw.astype(f32)
    values_flipped = flip(values, "xl")
    both = jnp.stack([q_raw, k_raw]).astype(f32)
    squares = jnp.sum(both * both, axis=2)
    cosine, signed_sine = rotation(positions, heads)
    squares = squares + flip(squares, "c")
    squares, cotangent = lax.optimization_barrier((squares, cotangent))
    inverse = lax.rsqrt((squares + flip(squares, "xh")) / inner_width + EPSILON)
    q_normed = q_float * inverse[0][:, None]
    k_normed = k_float * inverse[1][:, None]
    q_rot, k_rot = (
        (
            (factor * inverse[row])[:, None]
            * (raw.astype(f32) * cosine + partner_of(raw) * signed_sine)
        ).astype(jnp.bfloat16)
        for row, (raw, factor) in enumerate(((q_raw, 1.0), (k_raw, SCALING * LOG2E)))
    )
    gate_row = lax.dynamic_slice_in_dim(modulation, step_index[0], 1, 0)
    gated_cot = (gate_row * cotangent.astype(f32)).astype(jnp.bfloat16)
    attn_cot = lax.dot_general(
        gated_cot, out_weight, NT, preferred_element_type=f32
    ).astype(jnp.bfloat16)

    index = jnp.stack([lax.axis_index("z"), lax.axis_index("y"), lax.axis_index("xl")])
    queries = ring_gather(jnp.concatenate([q_rot, attn_cot], axis=1))
    keys = plane_gather(
        jnp.concatenate([k_rot, values], axis=1),
        jnp.concatenate([flip(k_rot, "xl"), values_flipped], axis=1),
    )

    places = list(range(8))
    stats = block_stats(index, places, queries, keys, heads)
    stats = merge([stats, swap(stats, "z", 1)], heads)
    stats = merge([stats] + [swap(stats, "z", mask) for mask in (2, 4, 6)], heads)
    top, total, weight = (stats[:, kind * heads : (kind + 1) * heads] for kind in range(3))
    rest = jnp.zeros((8, 16 - 2 * heads, 128), f32)
    totals = jnp.concatenate([top + jnp.log2(total), weight / total, rest], axis=1)

    dq, dkv = block_grads(index, places, queries, keys, totals, heads)
    dq_sum = ring_reduce(dq)
    dkv_sum = jnp.sum(lax.all_to_all(dkv, ("xl", "y"), 0, 0, tiled=True).astype(f32), axis=0)

    dq_normed = rotate(dq_sum, cosine, signed_sine, -1.0)
    dk_normed = rotate(dkv_sum[0], cosine, signed_sine, -1.0)
    slopes = jnp.stack(
        [jnp.sum(dq_normed * q_normed, axis=1), jnp.sum(dk_normed * k_normed, axis=1)]
    )
    slopes = sum_heads_axes(slopes) / inner_width
    query_grad = inverse[0][:, None] * (dq_normed - q_normed * slopes[0][:, None])
    key_grad = inverse[1][:, None] * (dk_normed - k_normed * slopes[1][:, None])
    return (
        query_grad.astype(jnp.bfloat16),
        key_grad.astype(jnp.bfloat16),
        dkv_sum[1].astype(jnp.bfloat16),
    )


def solution(mesh):
    axes = ("xl", "z", "y", "xh", "c")
    fine = Mesh(np.asarray(mesh.devices).reshape(2, 8, 4, 2, 2), axes)
    split = P(TOKENS_AXES, HEADS_AXES)
    rows = P(TOKENS_AXES, None)
    return jax.shard_map(
        shards,
        mesh=fine,
        in_specs=(split, split, split, rows, rows, P(HEADS_AXES, None), P(), P()),
        out_specs=(split, split, split),
        check_vma=False,
    )
```

```python
import functools
import math

import jax
import jax.numpy as jnp
import numpy as np
from jax import lax
from jax.experimental import pallas as pl
from jax.experimental.pallas import tpu as pltpu
from jax.sharding import Mesh
from jax.sharding import PartitionSpec as P

HEAD_DIM = 128
EPSILON = 1e-06
LOG2E = math.log2(math.e)
SCALING = 1.0 / math.sqrt(HEAD_DIM)
TOKENS_AXES = ("xl", "z", "y")
HEADS_AXES = ("xh", "c")
VMEM_LIMIT = 58 * 1024 * 1024
NT = (((1,), (1,)), ((), ()))
TN = (((0,), (0,)), ((), ()))


def angle_table(head_size):
    side_dim = 2 * (head_size // 6)
    first_dim = head_size - 2 * side_dim
    freq_table = np.zeros((3, head_size // 2), np.float32)
    column = 0
    for axis_number, group_dim in enumerate([first_dim, side_dim, side_dim]):
        for pair_index in range(group_dim // 2):
            freq_table[axis_number, column] = 10000.0 ** (-2.0 * pair_index / group_dim)
            column += 1
    return freq_table


def rotation(positions, heads_count):
    table = np.repeat(angle_table(HEAD_DIM), 2, axis=1)
    place = positions.astype(jnp.float32)
    angles = sum(place[:, axis : axis + 1] * jnp.asarray(table[axis])[None, :] for axis in range(3))
    parity = jnp.asarray(np.tile(np.array([-1.0, 1.0], np.float32), HEAD_DIM // 2))
    cosine, signed_sine = lax.optimization_barrier(
        (jnp.cos(angles), jnp.sin(angles) * parity[None, :])
    )
    return (
        jnp.concatenate([cosine] * heads_count, axis=1),
        jnp.concatenate([signed_sine] * heads_count, axis=1),
    )


def partner_of(source):
    columns = np.arange(source.shape[1])
    exchange = (columns[:, None] == (columns ^ 1)[None, :]).astype(np.float32)
    return jnp.dot(
        source, jnp.asarray(exchange, dtype=jnp.bfloat16), preferred_element_type=jnp.float32
    )


def rotate(source, cosine, signed_sine, direction):
    column_ids = jnp.arange(source.shape[1])
    partner = jnp.where(
        column_ids % 2 == 0, jnp.roll(source, -1, axis=1), jnp.roll(source, 1, axis=1)
    )
    return source * cosine + direction * partner * signed_sine


def shift(x, axis, distance):
    size = lax.axis_size(axis)
    return lax.ppermute(x, axis, [(i, (i + distance) % size) for i in range(size)])


def swap(x, axis, mask):
    return lax.ppermute(x, axis, [(i, i ^ mask) for i in range(lax.axis_size(axis))])


def other_pairs():
    beside = [(i, (i + 1) % 8 if i % 2 else (i - 1) % 8) for i in range(8)]
    beyond = [(i, (i + 2) % 8 if i % 2 else (i - 2) % 8) for i in range(8)]
    opposite = [(i, (i - 5) % 8 if i % 2 else (i + 5) % 8) for i in range(8)]
    return opposite, beyond, beside


def flip(x, axis):
    return lax.ppermute(x, axis, [(0, 1), (1, 0)])


def sum_heads_axes(x):
    total = x
    for mask in (1, 2, 3):
        total = total + lax.ppermute(x, HEADS_AXES, [(i, i ^ mask) for i in range(4)])
    return total


def ring_gather(x):
    half = x.shape[0] // 2
    left, right = x, x
    from_left, from_right = [], []
    for _ in range(3):
        left, right = shift(left, "z", 1), shift(right, "z", -1)
        from_left.append(left)
        from_right.append(right)
    far = [shift(left[:half], "z", 1), shift(right[half:], "z", -1)]
    return [[x], *[[b] for b in from_left], far, *[[b] for b in from_right[::-1]]]


def ring_reduce(blocks):
    half = blocks[4].shape[0] // 2
    low, high = shift(blocks[4][:half], "z", -2), shift(blocks[4][half:], "z", 2)
    left = (
        blocks[2]
        + shift(blocks[3], "z", -1)
        + jnp.concatenate([low, jnp.zeros_like(low)], axis=0)
    )
    right = (
        blocks[6]
        + shift(blocks[5], "z", 1)
        + jnp.concatenate([jnp.zeros_like(high), high], axis=0)
    )
    left = blocks[1] + shift(left, "z", -1)
    right = blocks[7] + shift(right, "z", 1)
    f32 = jnp.float32
    return (
        blocks[0].astype(f32)
        + shift(left, "z", -1).astype(f32)
        + shift(right, "z", 1).astype(f32)
    )


def plane_gather(x, flipped):
    rows = x.shape[0]
    pair = jnp.concatenate([x, flipped], axis=0)
    left, right = shift(pair, "y", 1), shift(pair, "y", -1)
    low, high = shift(left[:rows], "y", 1), shift(right[rows:], "y", -1)
    return [pair, left, low, high, right]


def fill(target, refs):
    row = 0
    for ref in refs:
        count = ref.shape[0]
        target[row : row + count, :] = ref[...]
        row += count


def owner_of(index_ref, place):
    return lax.rem(index_ref[0] + 8 - place, 8)


def key_owner_of(index_ref, place):
    d, a = divmod(place, 2)
    return 4 * lax.rem(index_ref[2] + a, 2) + lax.rem(index_ref[1] + 4 - d, 4)


def split(refs, counts):
    out, first = [], 0
    for count in counts:
        out.append(refs[first : first + count])
        first += count
    return out, refs[first:]


def stats_kernel(places, counts, heads, index_ref, *refs):
    sides, (stats_ref, *scratch) = split(refs, counts)
    for target, side in zip(scratch, sides):
        fill(target, side)
    q_ref, c_ref, k_ref, v_ref = scratch
    h = pl.program_id(0)
    for t in range(0, len(places), 4):
        cols = slice(t * 128, t * 128 + 512)
        s = lax.dot_general(k_ref[...], q_ref[cols, :], NT, preferred_element_type=jnp.float32)
        g = lax.dot_general(v_ref[...], c_ref[cols, :], NT, preferred_element_type=jnp.float32)
        top = jnp.max(s, axis=0, keepdims=True)
        e = jnp.exp2(s - top)
        total = jnp.sum(e, axis=0, keepdims=True)
        weight = jnp.sum(e * g, axis=0, keepdims=True)
        for side in range(4):
            owner = owner_of(index_ref, places[t + side])
            part = slice(side * 128, side * 128 + 128)
            for kind, row in enumerate((top, total, weight)):
                stats_ref[owner, pl.ds(heads * kind + h, 1), :] = row[:, part]


def grads_kernel(places, counts, heads, index_ref, *refs):
    sides, (totals_ref, *rest) = split(refs, counts)
    dq_refs, dkv_ref, scratch, (dk_ref, dv_ref) = rest[:8], rest[8], rest[9:13], rest[13:]
    for target, side in zip(scratch, sides):
        fill(target, side)
    q_ref, c_ref, k_ref, v_ref = scratch
    k_turned = k_ref[...].astype(jnp.float32).T.astype(jnp.bfloat16)
    h = pl.program_id(0)
    for t in range(0, len(places), 2):
        cols = slice(t * 128, t * 128 + 256)
        owners = [owner_of(index_ref, place) for place in places[t : t + 2]]
        log_total, delta = (
            jnp.concatenate(
                [totals_ref[owner, pl.ds(heads * kind + h, 1), :] for owner in owners], axis=1
            )
            for kind in (0, 1)
        )
        s = lax.dot_general(k_ref[...], q_ref[cols, :], NT, preferred_element_type=jnp.float32)
        g = lax.dot_general(v_ref[...], c_ref[cols, :], NT, preferred_element_type=jnp.float32)
        p = jnp.exp2(s - log_total)
        ds = (p * (g - delta)).astype(jnp.bfloat16)
        dv = jnp.dot(p.astype(jnp.bfloat16), c_ref[cols, :], preferred_element_type=jnp.float32)
        dk = jnp.dot(ds, q_ref[cols, :], preferred_element_type=jnp.float32)
        if t == 0:
            dv_ref[...] = dv
            dk_ref[...] = dk
        else:
            dv_ref[...] += dv
            dk_ref[...] += dk
        dq = jnp.dot(k_turned, ds, preferred_element_type=jnp.float32)
        dq = (dq / LOG2E).T.astype(jnp.bfloat16)
        dq_refs[t][...] = dq[:128]
        dq_refs[t + 1][...] = dq[128:]
    for place in range(8):
        owner = key_owner_of(index_ref, place)
        rows = slice(place * 128, place * 128 + 128)
        dkv_ref[owner, 0] = (dk_ref[rows, :] * SCALING).astype(jnp.bfloat16)
        dkv_ref[owner, 1] = dv_ref[rows, :].astype(jnp.bfloat16)


SMEM_SPEC = pl.BlockSpec(memory_space=pltpu.SMEM)
ROWS_SPEC = pl.BlockSpec((8, 16, 128), lambda h: (0, 0, 0))


def side_specs(pieces, first):
    return [
        pl.BlockSpec((piece.shape[0], HEAD_DIM), lambda h: (0, first + h)) for piece in pieces
    ]


def sides_of(blocks, keys, heads):
    pieces = [piece for block in blocks for piece in block]
    operands = [*pieces, *pieces, *keys, *keys]
    specs = []
    for side in (pieces, keys):
        for first in (0, heads):
            specs += side_specs(side, first)
    return operands, specs, [len(pieces)] * 2 + [len(keys)] * 2


def block_stats(index, places, blocks, keys, heads):
    operands, specs, counts = sides_of(blocks, keys, heads)
    rows = 128 * len(blocks)
    return pl.pallas_call(
        functools.partial(stats_kernel, places, counts, heads),
        grid=(heads,),
        out_shape=jax.ShapeDtypeStruct((8, 16, 128), jnp.float32),
        in_specs=[SMEM_SPEC, *specs],
        out_specs=ROWS_SPEC,
        scratch_shapes=[pltpu.VMEM((rows, HEAD_DIM), jnp.bfloat16)] * 2
        + [pltpu.VMEM((1024, HEAD_DIM), jnp.bfloat16)] * 2,
        compiler_params=pltpu.CompilerParams(vmem_limit_bytes=VMEM_LIMIT),
        cost_estimate=pl.CostEstimate(
            flops=heads * rows * 2**17 * 16, bytes_accessed=2**23, transcendentals=heads * rows * 2**10
        ),
        name="block_stats",
    )(index, *operands)


def block_grads(index, places, blocks, keys, totals, heads):
    operands, specs, counts = sides_of(blocks, keys, heads)
    rows = 128 * len(blocks)
    width = heads * HEAD_DIM
    outs = pl.pallas_call(
        functools.partial(grads_kernel, places, counts, heads),
        grid=(heads,),
        out_shape=[jax.ShapeDtypeStruct((128, width), jnp.bfloat16)] * 8
        + [jax.ShapeDtypeStruct((8, 2, 128, width), jnp.bfloat16)],
        in_specs=[SMEM_SPEC, *specs, ROWS_SPEC],
        out_specs=[pl.BlockSpec((128, HEAD_DIM), lambda h: (0, h))] * 8
        + [pl.BlockSpec((8, 2, 128, HEAD_DIM), lambda h: (0, 0, 0, h))],
        scratch_shapes=[pltpu.VMEM((rows, HEAD_DIM), jnp.bfloat16)] * 2
        + [pltpu.VMEM((1024, HEAD_DIM), jnp.bfloat16)] * 2
        + [pltpu.VMEM((1024, HEAD_DIM), jnp.float32)] * 2,
        compiler_params=pltpu.CompilerParams(vmem_limit_bytes=VMEM_LIMIT),
        cost_estimate=pl.CostEstimate(
            flops=heads * rows * 2**17 * 20, bytes_accessed=2**24, transcendentals=heads * rows * 2**10
        ),
        name="block_grads",
    )(index, *operands, totals)
    return outs[:8], outs[8]


def merge(parts, heads):
    tops = [
        jnp.concatenate([part[:, :heads]] * 3 + [part[:, : 16 - 3 * heads]], axis=1)
        for part in parts
    ]
    top = functools.reduce(jnp.maximum, tops)
    total = sum(part * jnp.exp2(own - top) for part, own in zip(parts, tops))
    return jnp.where(jnp.arange(16)[None, :, None] < heads, top, total)


def shards(q_raw, k_raw, values, positions, cotangent, out_weight, modulation, step_index):
    width = q_raw.shape[1]
    heads = width // HEAD_DIM
    inner_width = width * 4
    f32 = jnp.float32
    q_float = q_raw.astype(f32)
    k_float = k_raw.astype(f32)
    values_flipped = flip(values, "xl")
    both = jnp.stack([q_raw, k_raw]).astype(f32)
    squares = jnp.sum(both * both, axis=2)
    cosine, signed_sine = rotation(positions, heads)
    squares = squares + flip(squares, "c")
    squares, cotangent = lax.optimization_barrier((squares, cotangent))
    inverse = lax.rsqrt((squares + flip(squares, "xh")) / inner_width + EPSILON)
    q_normed = q_float * inverse[0][:, None]
    k_normed = k_float * inverse[1][:, None]
    q_rot, k_rot = (
        (
            (factor * inverse[row])[:, None]
            * (raw.astype(f32) * cosine + partner_of(raw) * signed_sine)
        ).astype(jnp.bfloat16)
        for row, (raw, factor) in enumerate(((q_raw, 1.0), (k_raw, SCALING * LOG2E)))
    )
    gate_row = lax.dynamic_slice_in_dim(modulation, step_index[0], 1, 0)
    gated_cot = (gate_row * cotangent.astype(f32)).astype(jnp.bfloat16)
    attn_cot = lax.dot_general(
        gated_cot, out_weight, NT, preferred_element_type=f32
    ).astype(jnp.bfloat16)

    index = jnp.stack([lax.axis_index("z"), lax.axis_index("y"), lax.axis_index("xl")])
    queries = ring_gather(jnp.concatenate([q_rot, attn_cot], axis=1))
    keys = plane_gather(
        jnp.concatenate([k_rot, values], axis=1),
        jnp.concatenate([flip(k_rot, "xl"), values_flipped], axis=1),
    )

    places = list(range(8))
    stats = block_stats(index, places, queries, keys, heads)
    stats = merge([stats, swap(stats, "z", 1)], heads)
    stats = merge([stats] + [lax.ppermute(stats, "z", perm) for perm in other_pairs()], heads)
    top, total, weight = (stats[:, kind * heads : (kind + 1) * heads] for kind in range(3))
    rest = jnp.zeros((8, 16 - 2 * heads, 128), f32)
    totals = jnp.concatenate([top + jnp.log2(total), weight / total, rest], axis=1)

    dq, dkv = block_grads(index, places, queries, keys, totals, heads)
    dq_sum = ring_reduce(dq)
    dkv_sum = jnp.sum(lax.all_to_all(dkv, ("xl", "y"), 0, 0, tiled=True).astype(f32), axis=0)

    dq_normed = rotate(dq_sum, cosine, signed_sine, -1.0)
    dk_normed = rotate(dkv_sum[0], cosine, signed_sine, -1.0)
    slopes = jnp.stack(
        [jnp.sum(dq_normed * q_normed, axis=1), jnp.sum(dk_normed * k_normed, axis=1)]
    )
    slopes = sum_heads_axes(slopes) / inner_width
    query_grad = inverse[0][:, None] * (dq_normed - q_normed * slopes[0][:, None])
    key_grad = inverse[1][:, None] * (dk_normed - k_normed * slopes[1][:, None])
    return (
        query_grad.astype(jnp.bfloat16),
        key_grad.astype(jnp.bfloat16),
        dkv_sum[1].astype(jnp.bfloat16),
    )


def solution(mesh):
    axes = ("xl", "z", "y", "xh", "c")
    fine = Mesh(np.asarray(mesh.devices).reshape(2, 8, 4, 2, 2), axes)
    split = P(TOKENS_AXES, HEADS_AXES)
    rows = P(TOKENS_AXES, None)
    return jax.shard_map(
        shards,
        mesh=fine,
        in_specs=(split, split, split, rows, rows, P(HEADS_AXES, None), P(), P()),
        out_specs=(split, split, split),
        check_vma=False,
    )
```

```python
import functools
import math

import jax
import jax.numpy as jnp
import numpy as np
from jax import lax
from jax.experimental import pallas as pl
from jax.experimental.pallas import tpu as pltpu
from jax.sharding import Mesh
from jax.sharding import PartitionSpec as P

HEAD_DIM = 128
EPSILON = 1e-06
LOG2E = math.log2(math.e)
SCALING = 1.0 / math.sqrt(HEAD_DIM)
TOKENS_AXES = ("xl", "z", "y")
HEADS_AXES = ("xh", "c")
VMEM_LIMIT = 58 * 1024 * 1024
NT = (((1,), (1,)), ((), ()))
TN = (((0,), (0,)), ((), ()))


def angle_table(head_size):
    side_dim = 2 * (head_size // 6)
    first_dim = head_size - 2 * side_dim
    freq_table = np.zeros((3, head_size // 2), np.float32)
    column = 0
    for axis_number, group_dim in enumerate([first_dim, side_dim, side_dim]):
        for pair_index in range(group_dim // 2):
            freq_table[axis_number, column] = 10000.0 ** (-2.0 * pair_index / group_dim)
            column += 1
    return freq_table


def rotation(positions, heads_count):
    table = np.repeat(angle_table(HEAD_DIM), 2, axis=1)
    place = positions.astype(jnp.float32)
    angles = sum(place[:, axis : axis + 1] * jnp.asarray(table[axis])[None, :] for axis in range(3))
    parity = jnp.asarray(np.tile(np.array([-1.0, 1.0], np.float32), HEAD_DIM // 2))
    cosine, signed_sine = lax.optimization_barrier(
        (jnp.cos(angles), jnp.sin(angles) * parity[None, :])
    )
    return (
        jnp.concatenate([cosine] * heads_count, axis=1),
        jnp.concatenate([signed_sine] * heads_count, axis=1),
    )


def partner_of(source):
    columns = np.arange(source.shape[1])
    exchange = (columns[:, None] == (columns ^ 1)[None, :]).astype(np.float32)
    return jnp.dot(
        source, jnp.asarray(exchange, dtype=jnp.bfloat16), preferred_element_type=jnp.float32
    )


def rotate(source, cosine, signed_sine, direction):
    column_ids = jnp.arange(source.shape[1])
    partner = jnp.where(
        column_ids % 2 == 0, jnp.roll(source, -1, axis=1), jnp.roll(source, 1, axis=1)
    )
    return source * cosine + direction * partner * signed_sine


def shift(x, axis, distance):
    size = lax.axis_size(axis)
    return lax.ppermute(x, axis, [(i, (i + distance) % size) for i in range(size)])


def swap(x, axis, mask):
    return lax.ppermute(x, axis, [(i, i ^ mask) for i in range(lax.axis_size(axis))])


def other_pairs():
    beside = [(i, (i + 1) % 8 if i % 2 else (i - 1) % 8) for i in range(8)]
    beyond = [(i, (i + 2) % 8 if i % 2 else (i - 2) % 8) for i in range(8)]
    opposite = [(i, (i - 5) % 8 if i % 2 else (i + 5) % 8) for i in range(8)]
    return opposite, beyond, beside


def flip(x, axis):
    return lax.ppermute(x, axis, [(0, 1), (1, 0)])


def sum_heads_axes(x):
    total = x
    for mask in (1, 2, 3):
        total = total + lax.ppermute(x, HEADS_AXES, [(i, i ^ mask) for i in range(4)])
    return total


def ring_gather(x):
    half = x.shape[0] // 2
    left, right = x, x
    from_left, from_right = [], []
    for _ in range(3):
        left, right = shift(left, "z", 1), shift(right, "z", -1)
        from_left.append(left)
        from_right.append(right)
    far = [shift(left[:half], "z", 1), shift(right[half:], "z", -1)]
    return [[x], *[[b] for b in from_left], far, *[[b] for b in from_right[::-1]]]


def ring_reduce(blocks):
    half = blocks[4].shape[0] // 2
    low, high = shift(blocks[4][:half], "z", -2), shift(blocks[4][half:], "z", 2)
    left = (
        blocks[2]
        + shift(blocks[3], "z", -1)
        + jnp.concatenate([low, jnp.zeros_like(low)], axis=0)
    )
    right = (
        blocks[6]
        + shift(blocks[5], "z", 1)
        + jnp.concatenate([jnp.zeros_like(high), high], axis=0)
    )
    left = blocks[1] + shift(left, "z", -1)
    right = blocks[7] + shift(right, "z", 1)
    f32 = jnp.float32
    return (
        blocks[0].astype(f32)
        + shift(left, "z", -1).astype(f32)
        + shift(right, "z", 1).astype(f32)
    )


def plane_gather(x, flipped):
    rows = x.shape[0]
    pair = jnp.concatenate([x, flipped], axis=0)
    left, right = shift(pair, "y", 1), shift(pair, "y", -1)
    low, high = shift(left[:rows], "y", 1), shift(right[rows:], "y", -1)
    return [pair, left, low, high, right]


def fill(target, refs):
    row = 0
    for ref in refs:
        count = ref.shape[0]
        target[row : row + count, :] = ref[...]
        row += count


def owner_of(index_ref, place):
    return lax.rem(index_ref[0] + 8 - place, 8)


def key_owner_of(index_ref, place):
    d, a = divmod(place, 2)
    return 4 * lax.rem(index_ref[2] + a, 2) + lax.rem(index_ref[1] + 4 - d, 4)


def split(refs, counts):
    out, first = [], 0
    for count in counts:
        out.append(refs[first : first + count])
        first += count
    return out, refs[first:]


def stats_kernel(places, counts, heads, index_ref, *refs):
    sides, (stats_ref, *scratch) = split(refs, counts)
    for target, side in zip(scratch, sides):
        fill(target, side)
    q_ref, c_ref, k_ref, v_ref = scratch
    h = pl.program_id(0)
    for t in range(0, len(places), 4):
        cols = slice(t * 128, t * 128 + 512)
        s = lax.dot_general(k_ref[...], q_ref[cols, :], NT, preferred_element_type=jnp.float32)
        g = lax.dot_general(v_ref[...], c_ref[cols, :], NT, preferred_element_type=jnp.float32)
        top = jnp.max(s, axis=0, keepdims=True)
        e = jnp.exp2(s - top)
        total = jnp.sum(e, axis=0, keepdims=True)
        weight = jnp.sum(e * g, axis=0, keepdims=True)
        for side in range(4):
            owner = owner_of(index_ref, places[t + side])
            part = slice(side * 128, side * 128 + 128)
            for kind, row in enumerate((top, total, weight)):
                stats_ref[owner, pl.ds(heads * kind + h, 1), :] = row[:, part]


def grads_kernel(places, counts, heads, index_ref, *refs):
    sides, (totals_ref, *rest) = split(refs, counts)
    dq_refs, dkv_ref, scratch, (dk_ref, dv_ref) = rest[:8], rest[8], rest[9:13], rest[13:]
    for target, side in zip(scratch, sides):
        fill(target, side)
    q_ref, c_ref, k_ref, v_ref = scratch
    k_turned = k_ref[...].astype(jnp.float32).T.astype(jnp.bfloat16)
    h = pl.program_id(0)
    for t in (0, 4):
        cols = slice(t * 128, t * 128 + 512)
        owners = [owner_of(index_ref, place) for place in places[t : t + 4]]
        log_total, delta = (
            jnp.concatenate(
                [totals_ref[owner, pl.ds(heads * kind + h, 1), :] for owner in owners], axis=1
            )
            for kind in (0, 1)
        )
        s = lax.dot_general(k_ref[...], q_ref[cols, :], NT, preferred_element_type=jnp.float32)
        g = lax.dot_general(v_ref[...], c_ref[cols, :], NT, preferred_element_type=jnp.float32)
        p = jnp.exp2(s - log_total)
        ds = (p * (g - delta)).astype(jnp.bfloat16)
        dv = jnp.dot(p.astype(jnp.bfloat16), c_ref[cols, :], preferred_element_type=jnp.float32)
        dk = jnp.dot(ds, q_ref[cols, :], preferred_element_type=jnp.float32)
        if t == 0:
            dv_ref[...] = dv
            dk_ref[...] = dk
        else:
            dv = (dv_ref[...] + dv).astype(jnp.bfloat16)
            dk = ((dk_ref[...] + dk) * SCALING).astype(jnp.bfloat16)
            for place in range(8):
                owner = key_owner_of(index_ref, place)
                rows = slice(place * 128, place * 128 + 128)
                dkv_ref[owner, 0] = dk[rows]
                dkv_ref[owner, 1] = dv[rows]
        dq = jnp.dot(k_turned, ds, preferred_element_type=jnp.float32)
        dq = (dq / LOG2E).T.astype(jnp.bfloat16)
        for side in range(4):
            dq_refs[t + side][...] = dq[side * 128 : side * 128 + 128]


SMEM_SPEC = pl.BlockSpec(memory_space=pltpu.SMEM)
ROWS_SPEC = pl.BlockSpec((8, 16, 128), lambda h: (0, 0, 0))


def side_specs(pieces, first):
    return [
        pl.BlockSpec((piece.shape[0], HEAD_DIM), lambda h: (0, first + h)) for piece in pieces
    ]


def sides_of(blocks, keys, heads):
    pieces = [piece for block in blocks for piece in block]
    operands = [*pieces, *pieces, *keys, *keys]
    specs = []
    for side in (pieces, keys):
        for first in (0, heads):
            specs += side_specs(side, first)
    return operands, specs, [len(pieces)] * 2 + [len(keys)] * 2


def block_stats(index, places, blocks, keys, heads):
    operands, specs, counts = sides_of(blocks, keys, heads)
    rows = 128 * len(blocks)
    return pl.pallas_call(
        functools.partial(stats_kernel, places, counts, heads),
        grid=(heads,),
        out_shape=jax.ShapeDtypeStruct((8, 16, 128), jnp.float32),
        in_specs=[SMEM_SPEC, *specs],
        out_specs=ROWS_SPEC,
        scratch_shapes=[pltpu.VMEM((rows, HEAD_DIM), jnp.bfloat16)] * 2
        + [pltpu.VMEM((1024, HEAD_DIM), jnp.bfloat16)] * 2,
        compiler_params=pltpu.CompilerParams(vmem_limit_bytes=VMEM_LIMIT),
        cost_estimate=pl.CostEstimate(
            flops=heads * rows * 2**17 * 16, bytes_accessed=2**23, transcendentals=heads * rows * 2**10
        ),
        name="block_stats",
    )(index, *operands)


def block_grads(index, places, blocks, keys, totals, heads):
    operands, specs, counts = sides_of(blocks, keys, heads)
    rows = 128 * len(blocks)
    width = heads * HEAD_DIM
    outs = pl.pallas_call(
        functools.partial(grads_kernel, places, counts, heads),
        grid=(heads,),
        out_shape=[jax.ShapeDtypeStruct((128, width), jnp.bfloat16)] * 8
        + [jax.ShapeDtypeStruct((8, 2, 128, width), jnp.bfloat16)],
        in_specs=[SMEM_SPEC, *specs, ROWS_SPEC],
        out_specs=[pl.BlockSpec((128, HEAD_DIM), lambda h: (0, h))] * 8
        + [pl.BlockSpec((8, 2, 128, HEAD_DIM), lambda h: (0, 0, 0, h))],
        scratch_shapes=[pltpu.VMEM((rows, HEAD_DIM), jnp.bfloat16)] * 2
        + [pltpu.VMEM((1024, HEAD_DIM), jnp.bfloat16)] * 2
        + [pltpu.VMEM((1024, HEAD_DIM), jnp.float32)] * 2,
        compiler_params=pltpu.CompilerParams(vmem_limit_bytes=VMEM_LIMIT),
        cost_estimate=pl.CostEstimate(
            flops=heads * rows * 2**17 * 20, bytes_accessed=2**24, transcendentals=heads * rows * 2**10
        ),
        name="block_grads",
    )(index, *operands, totals)
    return outs[:8], outs[8]


def merge(parts, heads):
    tops = [
        jnp.concatenate([part[:, :heads]] * 3 + [part[:, : 16 - 3 * heads]], axis=1)
        for part in parts
    ]
    top = functools.reduce(jnp.maximum, tops)
    total = sum(part * jnp.exp2(own - top) for part, own in zip(parts, tops))
    return jnp.where(jnp.arange(16)[None, :, None] < heads, top, total)


def shards(q_raw, k_raw, values, positions, cotangent, out_weight, modulation, step_index):
    width = q_raw.shape[1]
    heads = width // HEAD_DIM
    inner_width = width * 4
    f32 = jnp.float32
    q_float = q_raw.astype(f32)
    k_float = k_raw.astype(f32)
    values_flipped = flip(values, "xl")
    both = jnp.stack([q_raw, k_raw]).astype(f32)
    squares = jnp.sum(both * both, axis=2)
    cosine, signed_sine = rotation(positions, heads)
    squares = squares + flip(squares, "c")
    squares, cotangent = lax.optimization_barrier((squares, cotangent))
    inverse = lax.rsqrt((squares + flip(squares, "xh")) / inner_width + EPSILON)
    q_normed = q_float * inverse[0][:, None]
    k_normed = k_float * inverse[1][:, None]
    q_rot, k_rot = (
        (
            (factor * inverse[row])[:, None]
            * (raw.astype(f32) * cosine + partner_of(raw) * signed_sine)
        ).astype(jnp.bfloat16)
        for row, (raw, factor) in enumerate(((q_raw, 1.0), (k_raw, SCALING * LOG2E)))
    )
    gate_row = lax.dynamic_slice_in_dim(modulation, step_index[0], 1, 0)
    gated_cot = (gate_row * cotangent.astype(f32)).astype(jnp.bfloat16)
    attn_cot = lax.dot_general(
        gated_cot, out_weight, NT, preferred_element_type=f32
    ).astype(jnp.bfloat16)

    index = jnp.stack([lax.axis_index("z"), lax.axis_index("y"), lax.axis_index("xl")])
    queries = ring_gather(jnp.concatenate([q_rot, attn_cot], axis=1))
    keys = plane_gather(
        jnp.concatenate([k_rot, values], axis=1),
        jnp.concatenate([flip(k_rot, "xl"), values_flipped], axis=1),
    )

    places = list(range(8))
    stats = block_stats(index, places, queries, keys, heads)
    stats = merge([stats, swap(stats, "z", 1)], heads)
    stats = merge([stats] + [lax.ppermute(stats, "z", perm) for perm in other_pairs()], heads)
    top, total, weight = (stats[:, kind * heads : (kind + 1) * heads] for kind in range(3))
    rest = jnp.zeros((8, 16 - 2 * heads, 128), f32)
    totals = jnp.concatenate([top + jnp.log2(total), weight / total, rest], axis=1)

    dq, dkv = block_grads(index, places, queries, keys, totals, heads)
    dq_sum = ring_reduce(dq)
    dkv_sum = jnp.sum(lax.all_to_all(dkv, ("xl", "y"), 0, 0, tiled=True).astype(f32), axis=0)

    dq_normed = rotate(dq_sum, cosine, signed_sine, -1.0)
    dk_normed = rotate(dkv_sum[0], cosine, signed_sine, -1.0)
    slopes = jnp.stack(
        [jnp.sum(dq_normed * q_normed, axis=1), jnp.sum(dk_normed * k_normed, axis=1)]
    )
    slopes = sum_heads_axes(slopes) / inner_width
    query_grad = inverse[0][:, None] * (dq_normed - q_normed * slopes[0][:, None])
    key_grad = inverse[1][:, None] * (dk_normed - k_normed * slopes[1][:, None])
    return (
        query_grad.astype(jnp.bfloat16),
        key_grad.astype(jnp.bfloat16),
        dkv_sum[1].astype(jnp.bfloat16),
    )


def solution(mesh):
    axes = ("xl", "z", "y", "xh", "c")
    fine = Mesh(np.asarray(mesh.devices).reshape(2, 8, 4, 2, 2), axes)
    split = P(TOKENS_AXES, HEADS_AXES)
    rows = P(TOKENS_AXES, None)
    return jax.shard_map(
        shards,
        mesh=fine,
        in_specs=(split, split, split, rows, rows, P(HEADS_AXES, None), P(), P()),
        out_specs=(split, split, split),
        check_vma=False,
    )
```
